32 devices in a mesh: dp: 16 (over z, y, x), rep: 2 (over core).
Axes of the slice: x: 2, y: 2, z: 4, core: 2. Of those that a mesh axis runs over, the one named last changes fastest.
Arguments:
- tokens: bfloat16 [16384, 512], P(('dp', 'rep')), may hold values from -6 to 6
- memory: bfloat16 [16384, 512], P(('dp', 'rep')), may hold values from -6 to 6
- cotangent: bfloat16 [16384, 512], P(('dp', 'rep')), may hold values from -6 to 6
- lengths: int32 [32, 27], P(('dp', 'rep')), may hold values from 0 to 100, as said below
- blocks: float32 [256, 128, 128], P(('dp', 'rep')), may hold values from -0.53033009 to 0.53033009
- norm_params: float32 [3072], P(('dp', 'rep')), may hold values from -0.8 to 1.3
- graft_state: float32 [256, 128, 128], P(('dp', 'rep')), may hold values from 1024 to 4096
- left_stat: float32 [256, 128, 128], P(('dp', 'rep')), may hold values from -12582912 to 12582912, as said below
- right_stat: float32 [256, 128, 128], P(('dp', 'rep')), may hold values from -12582912 to 12582912, as said below
- left_root: float32 [256, 128, 128], P(('dp', 'rep')), may hold values from -0.15766808 to 0.15766808, as said below
- right_root: float32 [256, 128, 128], P(('dp', 'rep')), may hold values from -0.15766808 to 0.15766808, as said below
- norm_graft: float32 [3072], P(('dp', 'rep')), may hold values from 8192 to 32768
Outputs:
- decoded: bfloat16 [16384, 512], P(('dp', 'rep'))
- token_grad: float32 [16384, 512], P(('dp', 'rep'))
- memory_grad: float32 [16384, 512], P(('dp', 'rep'))
- block_grad: float32 [256, 128, 128], P(('dp', 'rep'))
- new_blocks: float32 [256, 128, 128], P(('dp', 'rep'))
- new_graft: float32 [256, 128, 128], P(('dp', 'rep'))
- new_left: float32 [256, 128, 128], P(('dp', 'rep'))
- new_right: float32 [256, 128, 128], P(('dp', 'rep'))
- norm_grad: float32 [3072], P(('dp', 'rep'))
- new_norms: float32 [3072], P(('dp', 'rep'))
- norm_moment: float32 [3072], P(('dp', 'rep'))
The draws below stay inside these ranges and needn't reach their ends.
Inputs may be any that keep to these rules, and one draw needn't show every extreme that they name: Live sentences come first in a row and empty slots hold 0; live lengths are 20 or more, and a row's lengths sum to at most 512. `left_stat`: every block is symmetric with a positive diagonal. `right_stat`: every block is symmetric with a positive diagonal. `left_root`: every block is symmetric with a positive diagonal. `right_root`: every block is symmetric with a positive diagonal.
All inputs are finite; a program needn't handle non-finite values.
Results may differ from the reference program's by a relative error of at most 0.035.
Values may be sent and summed in bfloat16 or wider, within the bound.
No kernel may reach another device: no remote copies, remote signals or barrier semaphores. Data moves between devices by JAX's collectives and lax.ppermute only.
A program may use at most 192 MiB of HBM per device.

```python
import math
import jax
import jax.numpy as jnp
from jax import lax

D = 512
HEADS = 8
FF = 2048
BLK = 128
NB = 256
TOK_DEV = 512
LEN_MIN = 20
LEN_MAX = 100
SENT_DEV = 27
TOKENS = 16384
N_DP = 16
N_REP = 2


def symmetric_blocks(key, magnitude, spread):
    streams = jax.random.split(key, 2)
    diagonal = magnitude * jnp.exp(jax.random.uniform(streams[0], (NB, BLK), minval=0.0, maxval=jnp.log(4.0)))
    normals = jax.random.truncated_normal(streams[1], -4.0, 4.0, (NB, BLK, BLK))
    mirrored = (normals + jnp.swapaxes(normals, 1, 2)) * (spread * magnitude / jnp.sqrt(2.0 * BLK))
    unit_diag = jnp.eye(BLK, dtype=jnp.float32)
    return (mirrored * (1.0 - unit_diag) + diagonal[:, :, None] * unit_diag).astype(jnp.float32)


def draw_lengths(key, part):
    key = jax.random.fold_in(key, 5)
    streams = jax.random.split(key, 5)
    row_count = N_DP * N_REP
    jitter = (LEN_MAX - LEN_MIN) // 10 + 1
    base_len = jax.random.randint(streams[0], (row_count, 1), LEN_MIN, LEN_MAX - jitter + 2)
    sent_lens = jnp.minimum(base_len + jax.random.randint(streams[1], (row_count, SENT_DEV), 0, jitter), LEN_MAX)
    longest = jax.random.randint(streams[2], (), 0, row_count)
    row_index = jnp.arange(row_count)[:, None]
    first_slot = jnp.arange(SENT_DEV)[None, :] == 0
    sent_lens = jnp.where((row_index == longest) & first_slot, LEN_MAX, sent_lens)
    capacity = jax.random.randint(streams[3], (row_count, 1), TOK_DEV // 2, TOK_DEV + 1)
    fullest = jax.random.randint(streams[4], (), 0, row_count)
    capacity = jnp.where(row_index == fullest, TOK_DEV, capacity)
    is_live = jnp.cumsum(sent_lens, axis=1) <= capacity
    return jnp.where(is_live, sent_lens, 0).astype(jnp.int32)


def draw_blocks(key, part):
    key = jax.random.fold_in(key, 7)
    per_side = D // BLK
    attn_count = 8 * per_side * per_side
    up_count = per_side * (FF // BLK)
    block_index = jnp.arange(NB)
    matrix = block_index // (per_side * per_side)
    attn_scale = jnp.where((matrix == 3) | (matrix == 7), 3.0, 1.0) / jnp.sqrt(1.0 * D)
    other_scale = jnp.where(block_index < attn_count + up_count, 1.0 / jnp.sqrt(1.0 * D), 1.0 / jnp.sqrt(1.0 * FF))
    magnitude = jnp.where(block_index < attn_count, attn_scale, other_scale)
    normals = jax.random.truncated_normal(key, -4.0, 4.0, (NB, BLK, BLK))
    return (normals * magnitude[:, None, None]).astype(jnp.float32)


def draw_norm_params(key, part):
    key = jax.random.fold_in(key, 9)
    streams = jax.random.split(key, 2)
    is_gain = jnp.arange(6 * D) // D % 2 == 0
    gains = 1.0 + jax.random.uniform(streams[0], (6 * D,), minval=-0.3, maxval=0.3)
    biases = 0.2 * jax.random.truncated_normal(streams[1], -4.0, 4.0, (6 * D,))
    return jnp.where(is_gain, gains, biases).astype(jnp.float32)


def draw_left_stat(key, part):
    key = jax.random.fold_in(key, 11)
    return symmetric_blocks(key, 1.0 * BLK * TOKENS, 1.0)


def draw_right_stat(key, part):
    key = jax.random.fold_in(key, 13)
    return symmetric_blocks(key, 1.0 * BLK * TOKENS, 1.0)


def draw_left_root(key, part):
    key = jax.random.fold_in(key, 17)
    return symmetric_blocks(key, (1.0 * BLK * TOKENS) ** (-0.25), 0.5)


def draw_right_root(key, part):
    key = jax.random.fold_in(key, 19)
    return symmetric_blocks(key, (1.0 * BLK * TOKENS) ** (-0.25), 0.5)


def levels(own_key, dims, cuts, low, top_value):
    def one(dim, blocks):
        draws = jax.random.uniform(jax.random.fold_in(jax.random.fold_in(own_key, 6), dim), (blocks,), jnp.float32, low / len(cuts), top_value / len(cuts))
        return jnp.repeat(jnp.exp(draws), dims[dim] // blocks).reshape((-1,) + (1,) * (len(dims) - dim - 1))

    level = one(*cuts[0])
    for cut in cuts[1:]:
        level = level * one(*cut)
    return level


def bell_draw(key, shape, scale, bound, shards=(), held_as=jnp.bfloat16):
    entries = jax.random.normal(key, shape, jnp.float32) * scale
    if len(shards) > 0:
        entries = levels(key, shape, shards, -0.22, 0.18) * entries
    return jnp.clip(entries, min=-bound, max=bound).astype(held_as)


def setup_inputs(seed: int = 0) -> dict:
    arg_keys = jax.random.split(jax.random.key(seed), 13)
    tokens = bell_draw(arg_keys[0], (TOKENS, D), 1.0, 6.0, ((0, 32),))
    memory = bell_draw(arg_keys[1], (TOKENS, D), 1.0, 6.0, ((0, 32),))
    cotangent = bell_draw(arg_keys[2], (TOKENS, D), 1.0, 6.0, ((0, 32),))
    lengths = draw_lengths(jax.random.fold_in(arg_keys[12], 71), 0)
    blocks = draw_blocks(jax.random.fold_in(arg_keys[12], 71), 0)
    norm_params = draw_norm_params(jax.random.fold_in(arg_keys[12], 71), 0)
    graft_state = jnp.clip(jnp.exp(math.log(4096.0) - 1.3862944 * jax.random.uniform(arg_keys[6], (NB, BLK, BLK), jnp.float32) ** levels(arg_keys[6], (NB, BLK, BLK), ((0, 32),), -0.2, 0.2)), 1024.0, 4096.0)
    left_stat = draw_left_stat(jax.random.fold_in(arg_keys[12], 71), 0)
    right_stat = draw_right_stat(jax.random.fold_in(arg_keys[12], 71), 0)
    left_root = draw_left_root(jax.random.fold_in(arg_keys[12], 71), 0)
    right_root = draw_right_root(jax.random.fold_in(arg_keys[12], 71), 0)
    norm_graft = jnp.clip(jnp.exp(math.log(32768.0) - 1.3862944 * jax.random.uniform(arg_keys[11], (6 * D,), jnp.float32) ** levels(arg_keys[11], (6 * D,), ((0, 32),), -0.2, 0.2)), 8192.0, 32768.0)
    return dict(tokens=tokens, memory=memory, cotangent=cotangent, lengths=lengths, blocks=blocks, norm_params=norm_params, graft_state=graft_state, left_stat=left_stat, right_stat=right_stat, left_root=left_root, right_root=right_root, norm_graft=norm_graft)


@jax.custom_vjp
def low(v):
    return lax.optimization_barrier(v.astype(jnp.bfloat16)).astype(jnp.float32)

@jax.custom_vjp
def low_back(v):
    return v

def low_keep(v):
    return (low(v), None)

def low_pass(kept, grad):
    return (grad,)

def back_keep(v):
    return (v, None)

def back_low(kept, grad):
    return (low(grad),)
low.defvjp(low_keep, low_pass)
low_back.defvjp(back_keep, back_low)
TOP_PRECISION = lax.Precision.HIGHEST
STAT_DECAY = 0.5
BLOCK_RATE = 0.05
NORM_RATE = 0.2
NORM_EPS = 1e-05
GRAFT_EPS = 1e-08
RATIO_EPS = 1e-06
MASKED = -1e+30

def to_mats(block_vals):
    per_side = D // BLK
    per_wide = FF // BLK
    attn_count = 8 * per_side * per_side
    attention = block_vals[:attn_count].reshape(8, per_side, per_side, BLK, BLK).transpose(0, 1, 3, 2, 4).reshape(8, D, D)
    up_proj = block_vals[attn_count:attn_count + per_side * per_wide].reshape(per_side, per_wide, BLK, BLK).transpose(0, 2, 1, 3).reshape(D, FF)
    down_proj = block_vals[attn_count + per_side * per_wide:].reshape(per_wide, per_side, BLK, BLK).transpose(0, 2, 1, 3).reshape(FF, D)
    return (attention, up_proj, down_proj)

def build_masks(sent_lens):
    bounds = jnp.cumsum(sent_lens.astype(jnp.int32)).astype(jnp.int32)
    position = jnp.arange(TOK_DEV, dtype=jnp.int32)
    segment = lax.optimization_barrier(jnp.sum((position[:, None] >= bounds[None, :]).astype(jnp.int32), axis=1))
    is_real = position < bounds[-1]
    segment = jnp.where(is_real, segment, -1)
    same_doc = segment[:, None] == segment[None, :]
    return (is_real, same_doc & (position[:, None] >= position[None, :]), same_doc)

def layer_norm(values, gain, bias):
    center = values - lax.optimization_barrier(jnp.mean(values, axis=-1, keepdims=True))
    spread = lax.optimization_barrier(jnp.mean(center * center, axis=-1, keepdims=True))
    return center * lax.rsqrt(spread + NORM_EPS) * gain + bias

def matmul(left_mat, right_mat):
    return jnp.dot(left_mat, right_mat, precision=TOP_PRECISION, preferred_element_type=jnp.float32)

def split_heads(values):
    return values.reshape(values.shape[0], HEADS, D // HEADS)

def attend(queries, key_rows, value_rows, mask):
    score_scale = (D // HEADS) ** (-0.5)
    scores = low_back(jnp.einsum('qhd,khd->hqk', split_heads(queries), split_heads(key_rows), precision=TOP_PRECISION) * score_scale)
    scores = jnp.where(mask[None], scores, MASKED)
    probs = low(jax.nn.softmax(scores, axis=-1))
    context = jnp.einsum('hqk,khd->qhd', probs, split_heads(value_rows), precision=TOP_PRECISION)
    return low(low_back(context.reshape(context.shape[0], D)))

def decoder_layer(inputs, attention, up_proj, down_proj, gains, mem_keys, mem_values, self_mask, cross_mask):
    inputs_low = low(inputs)
    queries = low(low_back(matmul(inputs_low, attention[0])))
    key_rows = low(low_back(matmul(inputs_low, attention[1])))
    value_rows = low(low_back(matmul(inputs_low, attention[2])))
    first_sum = inputs + low_back(matmul(attend(queries, key_rows, value_rows, self_mask), attention[3]))
    hidden_one = layer_norm(first_sum, gains[0], gains[1])
    cross_queries = low(low_back(matmul(low(hidden_one), attention[4])))
    second_sum = hidden_one + low_back(matmul(attend(cross_queries, mem_keys, mem_values, cross_mask), attention[7]))
    hidden_two = layer_norm(second_sum, gains[2], gains[3])
    pre_act = low_back(matmul(low(hidden_two), up_proj))
    third_sum = hidden_two + low_back(matmul(low(jax.nn.gelu(pre_act)), down_proj))
    return layer_norm(third_sum, gains[4], gains[5])

def shampoo_step(grad, weights, graft_state, left_stat, right_stat, left_root, right_root):

    def batched(first_mat, second_mat):
        return jnp.einsum('nij,njk->nik', first_mat, second_mat, precision=TOP_PRECISION)
    flipped = jnp.swapaxes(grad, 1, 2)
    new_left = STAT_DECAY * left_stat + (1.0 - STAT_DECAY) * batched(grad, flipped)
    new_right = STAT_DECAY * right_stat + (1.0 - STAT_DECAY) * batched(flipped, grad)
    new_graft = STAT_DECAY * graft_state + (1.0 - STAT_DECAY) * grad * grad
    direction = batched(batched(left_root, grad), right_root)
    adaptive = grad / (jnp.sqrt(new_graft) + GRAFT_EPS)
    ratio = jnp.sqrt(lax.optimization_barrier(jnp.mean(adaptive * adaptive, axis=(1, 2), keepdims=True))) * lax.rsqrt(lax.optimization_barrier(jnp.mean(direction * direction, axis=(1, 2), keepdims=True)) + RATIO_EPS)
    new_blocks = weights - BLOCK_RATE * ratio * direction
    return (new_blocks, new_graft, new_left, new_right)

def norm_step(grad, norm_params, norm_graft):
    moment = STAT_DECAY * norm_graft + (1.0 - STAT_DECAY) * grad * grad
    return (norm_params - NORM_RATE * grad / (jnp.sqrt(moment) + GRAFT_EPS), moment)

def reference(tokens, memory, cotangent, lengths, blocks, norm_params, graft_state, left_stat, right_stat, left_root, right_root, norm_graft):
    batches = N_DP * N_REP

    def forward(block_vals, norm_vals, token_vals, memory_vals):
        attention, up_proj, down_proj = to_mats(low(block_vals))
        gains = low(norm_vals).reshape(6, D)

        def one_batch(inputs):
            token_rows, memory_rows, sent_lens = inputs
            is_real, self_mask, cross_mask = build_masks(sent_lens)
            memory_low = low(memory_rows)
            mem_keys = low(low_back(matmul(memory_low, attention[5])))
            mem_values = low(low_back(matmul(memory_low, attention[6])))
            first_out = decoder_layer(token_rows, attention, up_proj, down_proj, gains, mem_keys, mem_values, self_mask, cross_mask)
            return decoder_layer(first_out, attention, up_proj, down_proj, gains, mem_keys, mem_values, self_mask, cross_mask)
        return lax.map(jax.checkpoint(one_batch), (token_vals.reshape(batches, TOK_DEV, D), memory_vals.reshape(batches, TOK_DEV, D), lengths))
    outputs, pullback = jax.vjp(forward, blocks, norm_params, tokens.astype(jnp.float32), memory.astype(jnp.float32))
    real_rows = (jnp.arange(TOK_DEV, dtype=jnp.int32)[None, :] < lax.optimization_barrier(jnp.sum(lengths, axis=1))[:, None]).astype(jnp.float32)[:, :, None]
    seed_grad = cotangent.astype(jnp.float32).reshape(batches, TOK_DEV, D) * real_rows
    block_grad, norm_grad, token_grad, memory_grad = pullback(seed_grad)
    decoded = (outputs * real_rows).astype(jnp.bfloat16).reshape(-1, D)
    new_blocks, new_graft, new_left, new_right = shampoo_step(block_grad, blocks, graft_state, left_stat, right_stat, left_root, right_root)
    new_norms, norm_moment = norm_step(norm_grad, norm_params, norm_graft)
    return (decoded, token_grad, memory_grad, block_grad, new_blocks, new_graft, new_left, new_right, norm_grad, new_norms, norm_moment)
```

```python
import functools
from typing import Any, NamedTuple

import jax
import jax.numpy as jnp
from jax import lax
from jax.experimental import pallas as pl
from jax.experimental.pallas import tpu as pltpu
from jax.sharding import PartitionSpec as P

D = 512
HEADS = 8
FF = 2048
BLK = 128
TOK_DEV = 512
PER_SIDE = D // BLK
PANELS = FF // D
PAIRS = HEADS // 2
HALF = 256

STAT_DECAY = 0.5
BLOCK_RATE = 0.05
NORM_RATE = 0.2
NORM_EPS = 1e-05
GRAFT_EPS = 1e-08
RATIO_EPS = 1e-06
MASKED = -1e30
SCALE = (D // HEADS) ** (-0.5)

AXES = ("dp", "rep")
F32 = jnp.float32
LOW = jnp.bfloat16
MAIN_VMEM = 60 * 2**20
PART_VMEM = 63 * 2**20 + 2**19

GRIDS = {16: (4, 2, 2)}

OWNERS = 32
OWN_BLOCKS = 8
OWN_NORMS = 96
OWN_ROWS = OWN_BLOCKS * BLK
PACK_ROWS = OWN_ROWS + 16

VM = pltpu.VMEM
WINDOWS_SELF = ((0, 256), (128, 384))
WINDOWS_CROSS = ((0, 512), (128, 384))
WINDOWS_ALL = ((0, 512), (0, 512))


def dot(left_mat, right_mat, left_dim, right_dim):
    return lax.dot_general(
        left_mat,
        right_mat,
        (((left_dim,), (right_dim,)), ((), ())),
        preferred_element_type=F32,
    )


def nn(left_mat, right_mat):
    return dot(left_mat, right_mat, 1, 0)


def nt(left_mat, right_mat):
    return dot(left_mat, right_mat, 1, 1)


def tn(left_mat, right_mat):
    return dot(left_mat, right_mat, 0, 0)


def matrix(wall, base, stride):
    def block(number):
        return wall[number * BLK : (number + 1) * BLK]

    rows = [
        jnp.concatenate([block(base + i * stride + j) for j in range(PER_SIDE)], axis=1)
        for i in range(PER_SIDE)
    ]
    return jnp.concatenate(rows, axis=0)


def attn_matrix(wall, which):
    return matrix(wall, which * PER_SIDE * PER_SIDE, PER_SIDE)


def up_panel(wall, panel):
    return matrix(wall, 128 + panel * PER_SIDE, FF // BLK)


def down_panel(wall, panel):
    return matrix(wall, 192 + panel * PER_SIDE * PER_SIDE, PER_SIDE)


def put_matrix(packs, base, stride, values):
    values = values.astype(packs.dtype)
    for i in range(PER_SIDE):
        for j in range(PER_SIDE):
            owner, place = divmod(base + i * stride + j, OWN_BLOCKS)
            first = owner * PACK_ROWS + place * BLK
            packs[first : first + BLK] = values[i * BLK : (i + 1) * BLK, j * BLK : (j + 1) * BLK]


def lanes_below(count, rows=1):
    return lax.broadcasted_iota(jnp.int32, (rows, BLK), 1) < count


def unpack_norms(packed, gains):
    turned = {shift: pltpu.roll(packed, shift, 1) for shift in (32, 64, 96)}
    turned[0] = packed
    for row in range(6 * D // BLK):
        owner, offset = divmod(row * BLK, OWN_NORMS)
        kept = OWN_NORMS - offset
        values = jnp.where(
            lanes_below(kept),
            turned[-offset % BLK][owner : owner + 1],
            turned[kept][owner + 1 : owner + 2],
        )
        gains[row // 4 : row // 4 + 1, (row % 4) * BLK : (row % 4 + 1) * BLK] = values


def pack_norms(gain_sum, flat, packs, first_owner, owners):
    for row in range(6 * D // BLK):
        flat[row : row + 1] = gain_sum[
            row // 4 : row // 4 + 1, (row % 4) * BLK : (row % 4 + 1) * BLK
        ]
    flat[24:32] = jnp.zeros((8, BLK), F32)
    values = flat[...]
    turned = {shift: pltpu.roll(values, shift, 1) for shift in (32, 64, 96)}
    turned[0] = values
    top = lax.broadcasted_iota(jnp.int32, (16, BLK), 0) == 0
    for owner in range(owners):
        row, offset = divmod((first_owner + owner) * OWN_NORMS, BLK)
        source = turned[-offset % BLK]
        mine = jnp.where(
            lanes_below(BLK - offset), source[row : row + 1], source[row + 1 : row + 2]
        )
        last = owner * PACK_ROWS + OWN_ROWS
        packs[last : last + 16] = jnp.where(top, mine, 0.0).astype(packs.dtype)


def norm_forward(values, gain, bias):
    center = values - jnp.mean(values, axis=1, keepdims=True)
    spread = jnp.mean(center * center, axis=1, keepdims=True)
    scale = lax.rsqrt(spread + NORM_EPS)
    unit = center * scale
    return unit * gain + bias, unit, scale


def norm_backward(grad, unit, scale, gain):
    inner = grad * gain
    first = jnp.mean(inner, axis=1, keepdims=True)
    second = jnp.mean(inner * unit, axis=1, keepdims=True)
    grad_in = (inner - first - unit * second) * scale
    grad_gain = jnp.sum(grad * unit, axis=0, keepdims=True)
    grad_bias = jnp.sum(grad, axis=0, keepdims=True)
    return grad_in, grad_gain, grad_bias


def chunks():
    return [pl.ds(start, HALF) for start in range(0, TOK_DEV, HALF)]


def pick_half(values, side):
    lane = lax.broadcasted_iota(jnp.int32, values.shape, 1)
    mine = lane < D // HEADS if side == 0 else lane >= D // HEADS
    return jnp.where(mine, values, jnp.zeros_like(values))


def both_halves(values, axis=0):
    return jnp.concatenate([pick_half(values, 0), pick_half(values, 1)], axis=axis)


def heads_wide(narrow):
    head_of = lax.broadcasted_iota(jnp.int32, (BLK, D), 1) // (D // HEADS)
    chooser = (head_of == lax.broadcasted_iota(jnp.int32, (BLK, D), 0)).astype(F32).astype(LOW)
    high = narrow.astype(LOW)
    rest = (narrow - high.astype(F32)).astype(LOW)
    return nn(
        jnp.concatenate([high, rest], axis=1), jnp.concatenate([chooser, chooser], axis=0)
    )


def for_pairs(total, windows, pair_step, copies=None):
    @pl.when(total >= BLK)
    def _():
        for pair in range(PAIRS):
            if copies is not None:
                copies.wait(pair)
            pair_step(windows, pair, pl.ds(pair * BLK, BLK))

    @pl.when(total < BLK)
    def _():
        if copies is not None:
            for pair in range(PAIRS):
                copies.wait(pair)

        def step(pair, carry):
            pair_step(WINDOWS_ALL, pair, pl.ds(pl.multiple_of(pair * BLK, BLK), BLK))
            return carry

        lax.fori_loop(0, PAIRS, step, 0)


def attend_forward(
    total, windows, queries, key_rows, value_rows, bias, probs, raw, inverse, context
):
    inverse[...] = jnp.zeros_like(inverse)

    def pair_step(spans, pair, lanes):
        for part, (start, size) in enumerate(spans):
            rows = pl.ds(part * HALF, HALF)
            span = pl.ds(start, size)
            query = queries[rows, lanes]
            keys = key_rows[span, lanes]
            values = value_rows[span, lanes]
            lane = lax.broadcasted_iota(jnp.int32, (size, BLK), 1)
            scores = [nt(keys, pick_half(query, side)) for side in range(2)]
            weights, sources = [], []
            for side in range(2):
                masked = scores[side] + bias[span, rows]
                top = jnp.max(masked, axis=0, keepdims=True)
                weight = jnp.exp(masked - top).astype(LOW)
                probs[2 * pair + side, span, rows] = weight
                weights.append(weight)
                ones = (lane == 2 * pair + side).astype(F32).astype(LOW)
                sources.append(jnp.concatenate([pick_half(values, side), ones], axis=1))
            mixed = tn(jnp.concatenate(weights, axis=0), jnp.concatenate(sources, axis=0))
            raw[rows, lanes] = mixed[:, :BLK]
            inverse[rows] += mixed[:, BLK:]

    for_pairs(total, windows, pair_step)
    for rows in chunks():
        sums = inverse[rows]
        narrow = jnp.where(sums > 0.0, 1.0 / sums, 0.0)
        inverse[rows] = narrow
        context[rows] = (raw[rows] * heads_wide(narrow)).astype(LOW)


def attend_backward(
    total, windows, queries, key_rows, value_rows, probs, inverse, context, grad_of,
    grad_context, inner_rows, grad_queries, put_keys, put_values, copies=None,
):
    head_of = lax.broadcasted_iota(jnp.int32, (16, D), 1) // (D // HEADS)
    chooser = (head_of == lax.broadcasted_iota(jnp.int32, (16, D), 0)).astype(F32).astype(LOW)
    for rows in chunks():
        grad = (grad_of(rows) * heads_wide(inverse[rows])).astype(LOW)
        grad_context[rows] = grad
        inner = grad.astype(F32) * context[rows].astype(F32)
        high = inner.astype(LOW)
        rest = (inner - high.astype(F32)).astype(LOW)
        inner_rows[:, rows] = nt(chooser, high) + nt(chooser, rest)

    def pair_step(spans, pair, lanes):
        shares = []
        for part, (start, size) in enumerate(spans):
            rows = pl.ds(part * HALF, HALF)
            span = pl.ds(start, size)
            keys = key_rows[span, lanes]
            values = value_rows[span, lanes]
            grad = grad_context[rows, lanes]
            weights = [probs[2 * pair + side, span, rows] for side in range(2)]
            grad_probs = [nt(values, pick_half(grad, side)) for side in range(2)]
            slopes = []
            for side in range(2):
                base = inner_rows[pl.ds(2 * pair + side, 1), rows]
                slopes.append((weights[side].astype(F32) * (grad_probs[side] - base)).astype(LOW))
            grad_queries[rows, lanes] = (
                tn(jnp.concatenate(slopes, axis=0), both_halves(keys)) * SCALE
            ).astype(LOW)
            shares.append(
                (
                    nn(jnp.concatenate(slopes, axis=1), both_halves(queries[rows, lanes])),
                    nn(jnp.concatenate(weights, axis=1), both_halves(grad)),
                )
            )
        for first in range(0, TOK_DEV, BLK):
            rows = pl.ds(first, BLK)
            for which, put in enumerate((put_keys, put_values)):
                parts = [
                    share[which][first - start : first - start + BLK]
                    for share, (start, size) in zip(shares, spans)
                    if start <= first < start + size
                ]
                put(rows, lanes, sum(parts[1:], parts[0]))

    for_pairs(total, windows, pair_step, copies)


def putter(target):
    def put(rows, lanes, values):
        target[rows, lanes] = values.astype(target.dtype)

    return put


def total_of(lengths):
    total = lengths[0, 0]
    for number in range(1, lengths.shape[1]):
        total = total + lengths[0, number]
    return total


def place_of(device):
    number = device[0]
    return number >> 3, (number >> 2) & 1, (number >> 1) & 1, number & 1


def make_biases(lengths, bias_self, bias_cross):
    count = lengths.shape[1]
    row = lax.broadcasted_iota(jnp.int32, (32, 1), 0)
    low = jnp.zeros((32, 1), jnp.int32)
    high = jnp.zeros((32, 1), jnp.int32)
    bound = jnp.int32(0)
    for number in range(count):
        low = jnp.where(row == number, bound, low)
        bound = bound + lengths[0, number]
        high = jnp.where(row == number, bound, high)
    low = jnp.where(row == count, bound, low)
    high = jnp.where(row == count, TOK_DEV, high)
    slot = lax.broadcasted_iota(jnp.int32, (32, TOK_DEV), 1)
    member = ((slot >= low) & (slot < high)).astype(F32).astype(LOW)
    for rows in chunks():
        apart = (tn(member, member[:, rows.start : rows.start + HALF]) - 1.0) * -MASKED
        key = lax.broadcasted_iota(jnp.int32, apart.shape, 0)
        query = lax.broadcasted_iota(jnp.int32, apart.shape, 1) + rows.start
        bias_cross[:, rows] = apart
        bias_self[:, rows] = jnp.where(key <= query, apart, MASKED)


class Shipping:
    def __init__(self, direct, device, packs, outs, sems):
        self.direct, self.packs, self.outs, self.sems = direct, packs, outs, sems
        _, self.y, self.x, self.core = place_of(device)
        self.waits = []

    def send(self, group, chip, core):
        number = (group * 4 + chip) * 2 + core
        source = self.packs.at[pl.ds(number * PACK_ROWS, PACK_ROWS)]
        sem = self.sems.at[number]
        if not self.direct:
            target = self.outs[0].at[pl.ds(number * PACK_ROWS, PACK_ROWS)]
            self.waits.append(pltpu.make_async_copy(source, target, sem))
            self.waits[-1].start()
            return
        move_y, move_x = self.y ^ (chip >> 1), self.x ^ (chip & 1)
        slot = move_x * 2 + move_y if core == 0 else move_y * 2 + move_x
        keep = pltpu.make_async_copy(source, self.outs[0].at[slot, group], sem)
        away = pltpu.make_async_copy(source, self.outs[1].at[slot, group], sem)

        @pl.when(self.core == core)
        def _():
            keep.start()

        @pl.when(self.core != core)
        def _():
            away.start()

        self.waits.append(keep)

    def send_chip(self, chip):
        for core in range(2):
            self.send(0, chip, core)

    def finish(self):
        for copy in self.waits:
            copy.wait()


def grad_shapes(direct, groups):
    if direct:
        return [jax.ShapeDtypeStruct((4, groups, PACK_ROWS, BLK), LOW)] * 2
    return [jax.ShapeDtypeStruct((groups * 8 * PACK_ROWS, BLK), LOW)]


LOW_SQ = ((TOK_DEV, D), LOW)
F32_SQ = ((TOK_DEV, D), F32)
COLUMN = ((TOK_DEV, 1), F32)
PER_HEAD = ((TOK_DEV, BLK), F32)
PROBS = ((HEADS, TOK_DEV, TOK_DEV), LOW)
WALL64 = ((64 * BLK, BLK), LOW)
PACKS8 = ((8 * PACK_ROWS, BLK), LOW)
WIDE = ((TOK_DEV, FF), LOW)
GAINS = ((8, D), F32)
INNER = ((16, TOK_DEV), F32)
FLAT = ((32, BLK), F32)


class Saved(NamedTuple):
    wall_self: Any = WALL64
    wall_cross: Any = WALL64
    probs_self: Any = PROBS
    probs_cross: Any = PROBS
    inverse_self: Any = PER_HEAD
    inverse_cross: Any = PER_HEAD
    queries: Any = LOW_SQ
    keys: Any = LOW_SQ
    values: Any = LOW_SQ
    context: Any = LOW_SQ
    hidden_one: Any = LOW_SQ
    cross_queries: Any = LOW_SQ
    cross_context: Any = LOW_SQ
    unit_one: Any = F32_SQ
    scale_one: Any = COLUMN
    mem_keys: Any = LOW_SQ
    mem_values: Any = LOW_SQ
    grad_second: Any = F32_SQ
    cross_branch: Any = LOW_SQ
    inputs_b: Any = LOW_SQ
    context_b: Any = LOW_SQ
    hidden_one_b: Any = LOW_SQ
    cross_context_b: Any = LOW_SQ
    cross_branch_b: Any = LOW_SQ
    cross_grad_b: Any = LOW_SQ
    self_branch_b: Any = LOW_SQ
    query_grad_b: Any = LOW_SQ
    key_grad_b: Any = LOW_SQ
    value_grad_b: Any = LOW_SQ
    mem_key_grad_b: Any = F32_SQ
    mem_value_grad_b: Any = F32_SQ


class Held(NamedTuple):
    tokens: Any = LOW_SQ
    memory: Any = LOW_SQ
    cotangent: Any = LOW_SQ
    bias_self: Any = F32_SQ
    bias_cross: Any = F32_SQ
    wall: Any = ((256 * BLK, BLK), LOW)
    norms: Any = ((OWNERS, 16, BLK), LOW)
    flat: Any = FLAT
    probs_self: Any = PROBS
    probs_cross: Any = PROBS
    inverse_self: Any = PER_HEAD
    inverse_cross: Any = PER_HEAD
    mem_keys: Any = LOW_SQ
    mem_values: Any = LOW_SQ
    state: Any = F32_SQ
    hidden: Any = F32_SQ
    grad_context: Any = LOW_SQ
    inner_rows: Any = INNER
    key_sum: Any = F32_SQ
    value_sum: Any = F32_SQ
    grad_second: Any = F32_SQ


class BothApps(NamedTuple):
    inputs: Any = LOW_SQ
    queries: Any = LOW_SQ
    keys: Any = LOW_SQ
    values: Any = LOW_SQ
    context: Any = LOW_SQ
    unit_one: Any = F32_SQ
    scale_one: Any = COLUMN
    hidden_one: Any = LOW_SQ
    cross_queries: Any = LOW_SQ
    cross_context: Any = LOW_SQ


class PerApp(NamedTuple):
    unit_two: Any = F32_SQ
    scale_two: Any = COLUMN
    hidden_two: Any = LOW_SQ
    gelu_slope: Any = WIDE
    activated: Any = WIDE
    unit_three: Any = F32_SQ
    scale_three: Any = COLUMN
    down_branch: Any = LOW_SQ


class Branches(NamedTuple):
    cross_branch: Any = LOW_SQ
    cross_grad: Any = LOW_SQ
    self_branch: Any = LOW_SQ
    query_grad: Any = LOW_SQ
    key_grad: Any = LOW_SQ
    value_grad: Any = LOW_SQ


def gelu_parts(values):
    first = 0.7978845608028654
    cubic = 0.044715 * first
    square = values * values
    bend = jnp.tanh(values * (first + cubic * square))
    half = 0.5 + 0.5 * bend
    slope = half + (0.5 * values) * (1.0 - bend * bend) * (first + (3.0 * cubic) * square)
    return values * half, slope


def attend_self(app, held, bias, total):
    weights = [attn_matrix(held.wall, which) for which in range(3)]
    for rows in chunks():
        inputs = held.state[rows].astype(LOW)
        app.inputs[rows] = inputs
        app.queries[rows] = (nn(inputs, weights[0]) * SCALE).astype(LOW)
        app.keys[rows] = nn(inputs, weights[1]).astype(LOW)
        app.values[rows] = nn(inputs, weights[2]).astype(LOW)
    attend_forward(
        total, WINDOWS_SELF, app.queries, app.keys, app.values, bias, held.probs_self,
        held.hidden, held.inverse_self, app.context,
    )


def finish_self(app, held, gains):
    weight = attn_matrix(held.wall, 3)
    for rows in chunks():
        total_rows = held.state[rows] + nn(app.context[rows], weight)
        out, unit, scale = norm_forward(total_rows, gains[0:1], gains[1:2])
        app.unit_one[rows] = unit
        app.scale_one[rows] = scale
        app.hidden_one[rows] = out.astype(LOW)
        held.hidden[rows] = out


def forward_cross(app, held, gains, bias, total):
    weight = attn_matrix(held.wall, 4)
    for rows in chunks():
        app.cross_queries[rows] = (nn(app.hidden_one[rows], weight) * SCALE).astype(LOW)
    attend_forward(
        total, WINDOWS_CROSS, app.cross_queries, held.mem_keys, held.mem_values, bias,
        held.probs_cross, held.state, held.inverse_cross, app.cross_context,
    )
    weight = attn_matrix(held.wall, 7)
    for rows in chunks():
        total_rows = held.hidden[rows] + nn(app.cross_context[rows], weight)
        out, unit, scale = norm_forward(total_rows, gains[2:3], gains[3:4])
        app.unit_two[rows] = unit
        app.scale_two[rows] = scale
        app.hidden_two[rows] = out.astype(LOW)
        held.hidden[rows] = out


def forward_mix(app, held, gains, finish):
    for rows in chunks():
        mixed = app.hidden_two[rows]
        total_rows = held.hidden[rows]
        for panel in range(PANELS):
            lanes = pl.ds(panel * D, D)
            active, slope = gelu_parts(nn(mixed, up_panel(held.wall, panel)))
            active = active.astype(LOW)
            app.activated[rows, lanes] = active
            app.gelu_slope[rows, lanes] = slope.astype(LOW)
            total_rows = total_rows + nn(active, down_panel(held.wall, panel))
        out, unit, scale = norm_forward(total_rows, gains[4:5], gains[5:6])
        app.unit_three[rows] = unit
        app.scale_three[rows] = scale
        finish(rows, out)


def backward_mix(app, held, gains, gain_sum, grad_of, branch):
    for rows in chunks():
        grad_third, gain3, bias3 = norm_backward(
            grad_of(rows), app.unit_three[rows], app.scale_three[rows], gains[4:5]
        )
        gain_sum[4:5] += gain3
        gain_sum[5:6] += bias3
        grad_low = grad_third.astype(LOW)
        app.down_branch[rows] = grad_low
        for panel in range(PANELS):
            lanes = pl.ds(panel * D, D)
            grad_active = nt(grad_low, down_panel(held.wall, panel))
            grad_pre = (grad_active * app.gelu_slope[rows, lanes].astype(F32)).astype(LOW)
            app.gelu_slope[rows, lanes] = grad_pre
            grad_third = grad_third + nt(grad_pre, up_panel(held.wall, panel))
        grad_in, gain2, bias2 = norm_backward(
            grad_third, app.unit_two[rows], app.scale_two[rows], gains[2:3]
        )
        gain_sum[2:3] += gain2
        gain_sum[3:4] += bias2
        held.grad_second[rows] = grad_in
        branch[rows] = grad_in.astype(LOW)


def backward_cross_end(app, weight, gains, gain_sum, grad_second, cross_grad, grad_first,
                       self_branch):
    for rows in chunks():
        grad = grad_second[rows] + nt(cross_grad[rows], weight)
        grad_in, gain1, bias1 = norm_backward(
            grad, app.unit_one[rows], app.scale_one[rows], gains[0:1]
        )
        gain_sum[0:1] += gain1
        gain_sum[1:2] += bias1
        grad_first[rows] = grad_in
        self_branch[rows] = grad_in.astype(LOW)


def layers_kernel(direct, piece_count, *refs):
    refs = list(refs)

    def take(table):
        count = table if isinstance(table, int) else len(table)
        taken, refs[:count] = refs[:count], []
        return taken if isinstance(table, int) else type(table)(*taken)

    device, lengths, tokens, memory, cotangent = take(5)
    gains_in = [] if direct else take(1)
    pieces = take(piece_count)
    decoded, gains, gain_sum = take(3)
    grad_outs = take(2 if direct else 1)
    saved = take(Saved())
    held = take(Held())
    both = take(BothApps())
    app_a, app_b, branches = take(PerApp()), take(PerApp()), take(Branches())
    piece_sem, input_sem, save_sem, ship_sem = take(4)

    class App(NamedTuple):
        inputs: Any
        queries: Any
        keys: Any
        values: Any
        context: Any
        unit_one: Any
        scale_one: Any
        hidden_one: Any
        cross_queries: Any
        cross_context: Any
        unit_two: Any
        scale_two: Any
        hidden_two: Any
        gelu_slope: Any
        activated: Any
        unit_three: Any
        scale_three: Any
        down_branch: Any

    app_a, app_b = App(*both, *app_a), App(*both, *app_b)
    wall = held.wall
    total = total_of(lengths)
    inputs = [
        pltpu.make_async_copy(source, target, input_sem.at[number])
        for number, (source, target) in enumerate(
            ((tokens, held.tokens), (memory, held.memory), (cotangent, held.cotangent))
        )
    ]
    inputs[0].start()
    if direct:
        arrive = fetch_pieces(device, pieces, wall, held.norms, piece_sem)
    else:
        whole = pltpu.make_async_copy(pieces[0], wall, piece_sem.at[0])
        whole.start()

        def arrive(group):
            if group == 0:
                whole.wait()

    for load in inputs[1:]:
        load.start()
    bias_self, bias_cross = held.bias_self, held.bias_cross
    make_biases(lengths, bias_self, bias_cross)
    gain_sum[...] = jnp.zeros_like(gain_sum)
    inputs[0].wait()
    memory, cotangent = held.memory, held.cotangent
    for rows in chunks():
        held.state[rows] = held.tokens[rows].astype(F32)
    arrive(0)

    stores = {}

    def save(target, source):
        number = len(stores)
        stores[number] = pltpu.make_async_copy(source, target, save_sem.at[number])
        stores[number].start()
        return number

    def settle(numbers):
        for number in numbers:
            stores[number].wait()

    walls = [save(saved.wall_self, wall.at[pl.ds(0, 64 * BLK)])]
    later = []
    gains[6:8] = jnp.zeros((2, D), F32)

    real = {
        start: lax.broadcasted_iota(jnp.int32, (HALF, 1), 0) + start < total
        for start in range(0, TOK_DEV, HALF)
    }

    def keep_state(rows, out):
        held.state[rows] = out

    def keep_decoded(rows, out):
        decoded[rows] = jnp.where(real[rows.start], out, 0.0).astype(LOW)

    attend_self(app_a, held, bias_self, total)
    arrive(1)
    arrive(2)
    arrive(3)
    if direct:
        for owner in range(OWNERS):
            held.flat[owner : owner + 1] = held.norms[owner].astype(F32)[0:1]
        unpack_norms(held.flat[...], gains)
    else:
        gains[...] = gains_in[0][...]
    walls.append(save(saved.wall_cross, wall.at[pl.ds(64 * BLK, 64 * BLK)]))
    for load in inputs[1:]:
        load.wait()
    weights = [attn_matrix(wall, which) for which in (5, 6)]
    for rows in chunks():
        held.mem_keys[rows] = nn(memory[rows], weights[0]).astype(LOW)
        held.mem_values[rows] = nn(memory[rows], weights[1]).astype(LOW)
    later += [save(saved.mem_keys, held.mem_keys), save(saved.mem_values, held.mem_values)]
    finish_self(app_a, held, gains)
    first_saves = [
        save(saved.probs_self, held.probs_self),
        save(saved.inverse_self, held.inverse_self),
        save(saved.queries, app_a.queries),
        save(saved.keys, app_a.keys),
        save(saved.values, app_a.values),
        save(saved.context, app_a.context),
        save(saved.hidden_one, app_a.hidden_one),
        save(saved.unit_one, app_a.unit_one),
        save(saved.scale_one, app_a.scale_one),
    ]
    forward_cross(app_a, held, gains, bias_cross, total)
    second_saves = [
        save(saved.probs_cross, held.probs_cross),
        save(saved.inverse_cross, held.inverse_cross),
        save(saved.cross_queries, app_a.cross_queries),
        save(saved.cross_context, app_a.cross_context),
    ]
    forward_mix(app_a, held, gains, keep_state)
    settle(first_saves)
    attend_self(app_b, held, bias_self, total)
    finish_self(app_b, held, gains)
    settle(second_saves)
    forward_cross(app_b, held, gains, bias_cross, total)
    forward_mix(app_b, held, gains, keep_decoded)
    later += [
        save(saved.inputs_b, app_b.inputs),
        save(saved.context_b, app_b.context),
        save(saved.hidden_one_b, app_b.hidden_one),
        save(saved.cross_context_b, app_b.cross_context),
    ]

    def last_grad(rows):
        return jnp.where(real[rows.start], cotangent[rows].astype(F32), 0.0)

    backward_mix(app_b, held, gains, gain_sum, last_grad, branches.cross_branch)
    later.append(save(saved.cross_branch_b, branches.cross_branch))
    weight = attn_matrix(wall, 7)
    attend_backward(
        total, WINDOWS_CROSS, app_b.cross_queries, held.mem_keys, held.mem_values,
        held.probs_cross, held.inverse_cross, app_b.cross_context,
        lambda rows: nt(branches.cross_branch[rows], weight), held.grad_context,
        held.inner_rows, branches.cross_grad, putter(held.key_sum), putter(held.value_sum),
    )
    later += [
        save(saved.mem_key_grad_b, held.key_sum),
        save(saved.mem_value_grad_b, held.value_sum),
        save(saved.cross_grad_b, branches.cross_grad),
    ]
    backward_cross_end(
        app_b, attn_matrix(wall, 4), gains, gain_sum, held.grad_second, branches.cross_grad,
        held.hidden, branches.self_branch,
    )
    later.append(save(saved.self_branch_b, branches.self_branch))
    weight_out = attn_matrix(wall, 3)
    attend_backward(
        total, WINDOWS_SELF, app_b.queries, app_b.keys, app_b.values, held.probs_self,
        held.inverse_self, app_b.context,
        lambda rows: nt(branches.self_branch[rows], weight_out), held.grad_context,
        held.inner_rows, branches.query_grad, putter(branches.key_grad),
        putter(branches.value_grad),
    )
    later += [
        save(saved.query_grad_b, branches.query_grad),
        save(saved.key_grad_b, branches.key_grad),
        save(saved.value_grad_b, branches.value_grad),
    ]
    weights = [attn_matrix(wall, which) for which in range(3)]
    for rows in chunks():
        held.state[rows] = (
            held.hidden[rows]
            + nt(branches.query_grad[rows], weights[0])
            + nt(branches.key_grad[rows], weights[1])
            + nt(branches.value_grad[rows], weights[2])
        )
    backward_mix(
        app_a, held, gains, gain_sum, lambda rows: held.state[rows], held.grad_context
    )
    later += [
        save(saved.grad_second, held.grad_second),
        save(saved.cross_branch, held.grad_context),
    ]

    settle(walls)
    packs = wall
    if direct:
        pack_norms(gain_sum, held.flat, packs, 16, 16)
    shipping = Shipping(direct, device, packs, grad_outs, ship_sem)
    for panel in range(PANELS):
        lanes = pl.ds(panel * D, D)
        put_matrix(
            packs, panel * PER_SIDE, FF // BLK,
            tn(app_a.hidden_two[...], app_a.gelu_slope[:, lanes])
            + tn(app_b.hidden_two[...], app_b.gelu_slope[:, lanes]),
        )
        if panel % 2 == 1:
            for chip in range(4):
                shipping.send(0, chip, panel // 2)
    for panel in range(PANELS):
        lanes = pl.ds(panel * D, D)
        put_matrix(
            packs, 64 + panel * PER_SIDE * PER_SIDE, PER_SIDE,
            tn(app_a.activated[:, lanes], app_a.down_branch[...])
            + tn(app_b.activated[:, lanes], app_b.down_branch[...]),
        )
        for core in range(2):
            shipping.send(1, panel, core)
    settle(later)
    shipping.finish()


def fetch_pieces(device, pieces, wall, norms, sems):
    z, y, x, core = place_of(device)
    copies = []
    for number, piece in enumerate(pieces):
        back, spot, other = number >> 3, (number >> 1) & 3, number & 1
        one, two = spot & 1, spot >> 1
        lane = core ^ other
        at_y = y ^ jnp.where(lane == 0, one, two)
        at_x = x ^ jnp.where(lane == 0, two, one)
        owner = ((((z - back) & 3) * 2 + at_y) * 2 + at_x) * 2 + lane
        copies.append(
            (
                pltpu.make_async_copy(
                    piece.at[pl.ds(0, OWN_ROWS)],
                    wall.at[pl.ds(pl.multiple_of(owner * OWN_ROWS, OWN_ROWS), OWN_ROWS)],
                    sems.at[2 * number],
                ),
                pltpu.make_async_copy(
                    piece.at[pl.ds(OWN_ROWS, 16)], norms.at[owner], sems.at[2 * number + 1]
                ),
            )
        )
    def for_plane(plane, act):
        for back in range(4):

            @pl.when(((z - plane) & 3) == back)
            def _(back=back):
                for pair in copies[back * 8 : back * 8 + 8]:
                    for copy in pair:
                        act(copy)

    def arrive(plane):
        for_plane(plane, lambda copy: copy.wait())
        if plane < 3:
            for_plane(plane + 1, lambda copy: copy.start())

    for_plane(0, lambda copy: copy.start())
    return arrive


class Loads:
    def __init__(self, names, sources, targets, sems):
        self.targets = dict(zip(names, targets))
        self.copies = {
            name: pltpu.make_async_copy(source, target, sems.at[number])
            for number, (name, source, target) in enumerate(zip(names, sources, targets))
        }

    def start(self):
        for copy in self.copies.values():
            copy.start()
        return self

    def __getattr__(self, name):
        if name in self.copies:
            self.copies.pop(name).wait()
        return self.targets[name]


class Stores:
    def __init__(self, names, sources, targets, sems):
        self.copies = {
            name: pltpu.make_async_copy(source, target, sems.at[number])
            for number, (name, source, target) in enumerate(zip(names, sources, targets))
        }

    def start(self, *names):
        for name in names:
            self.copies[name].start()

    def finish(self):
        for copy in self.copies.values():
            copy.wait()


def one_matrix(wall, which):
    return wall.at[pl.ds(which * 16 * BLK, 16 * BLK)]


class PairCopies:
    def __init__(self, source, target, sems, then):
        self.copies = [
            pltpu.make_async_copy(
                source.at[pl.ds(2 * pair, 2)], target.at[pl.ds(2 * pair, 2)], sems.at[pair]
            )
            for pair in range(PAIRS)
        ]
        self.copies[0].start()
        self.then = then

    def wait(self, pair):
        if pair == 0:
            for copy in self.copies[1:]:
                copy.start()
        self.copies[pair].wait()
        if pair == 1:
            self.then.start()


MATRIX = ((16 * BLK, BLK), LOW)


class CrossFirst(NamedTuple):
    cross_branch: Any = LOW_SQ
    weight_out: Any = MATRIX
    inverse_cross: Any = PER_HEAD
    cross_context: Any = LOW_SQ
    mem_keys: Any = LOW_SQ
    mem_values: Any = LOW_SQ
    cross_queries: Any = LOW_SQ


class CrossThen(NamedTuple):
    mem_key_grad_b: Any = F32_SQ
    mem_value_grad_b: Any = F32_SQ
    weight_query: Any = MATRIX
    grad_second: Any = F32_SQ
    unit_one: Any = F32_SQ
    scale_one: Any = COLUMN
    hidden_one: Any = LOW_SQ
    hidden_one_b: Any = LOW_SQ
    cross_grad_b: Any = LOW_SQ
    memory: Any = LOW_SQ
    cross_context_b: Any = LOW_SQ
    cross_branch_b: Any = LOW_SQ


class CrossOuts(NamedTuple):
    grad_first: Any = F32_SQ
    self_branch: Any = LOW_SQ
    gain_sum: Any = GAINS
    key_low: Any = LOW_SQ
    value_low: Any = LOW_SQ


class CrossWork(NamedTuple):
    probs: Any = PROBS
    key_sum: Any = F32_SQ
    value_sum: Any = F32_SQ
    grad_context: Any = LOW_SQ
    inner_rows: Any = INNER
    cross_grad: Any = LOW_SQ
    packs: Any = PACKS8
    flat: Any = FLAT


def split(refs, *parts):
    found, first = [], 0
    for part in parts:
        count = part if isinstance(part, int) else len(part)
        taken = refs[first : first + count]
        found.append(taken if isinstance(part, int) else type(part)(*taken))
        first += count
    return found


def cross_back_kernel(direct, device, lengths, gains, gain_before, order, *refs):
    first_in, probs_in, then_in, targets, grad_outs, first, then, outs, work, sems = split(
        refs, CrossFirst(), 1, CrossThen(), CrossOuts(), 2 if direct else 1, CrossFirst(),
        CrossThen(), CrossOuts(), CrossWork(), 5,
    )
    first_sem, then_sem, probs_sem, out_sem, ship_sem = sems
    stores = Stores(CrossOuts._fields, outs, targets, out_sem)
    loads = Loads(
        CrossFirst._fields, first_in._replace(weight_out=one_matrix(first_in.weight_out, 3)),
        first, first_sem,
    ).start()
    late = Loads(
        CrossThen._fields, then_in._replace(weight_query=one_matrix(then_in.weight_query, 0)),
        then, then_sem,
    )
    copies = PairCopies(probs_in[0], work.probs, probs_sem, late)
    outs.gain_sum[...] = gain_before[...]
    branch = loads.cross_branch
    weight = matrix(loads.weight_out, 0, PER_SIDE)
    inverse, context = loads.inverse_cross, loads.cross_context
    attend_backward(
        total_of(lengths), WINDOWS_CROSS, loads.cross_queries, loads.mem_keys,
        loads.mem_values, work.probs, inverse, context, lambda rows: nt(branch[rows], weight),
        work.grad_context, work.inner_rows, work.cross_grad, putter(work.key_sum),
        putter(work.value_sum), copies,
    )
    outs.key_low[...] = (work.key_sum[...] + late.mem_key_grad_b[...]).astype(LOW)
    outs.value_low[...] = (work.value_sum[...] + late.mem_value_grad_b[...]).astype(LOW)
    stores.start("key_low", "value_low")
    packs = work.packs
    shipping = Shipping(direct, device, packs, grad_outs, ship_sem)
    weight = matrix(late.weight_query, 0, PER_SIDE)
    grad_second = late.grad_second
    late.unit_one, late.scale_one
    backward_cross_end(
        late, weight, gains, outs.gain_sum, grad_second, work.cross_grad, outs.grad_first,
        outs.self_branch,
    )
    stores.start("grad_first", "self_branch", "gain_sum")
    if direct:
        pack_norms(outs.gain_sum, work.flat, packs, 8, 8)
    put_matrix(
        packs, 0, PER_SIDE,
        tn(late.hidden_one[...], work.cross_grad[...])
        + tn(late.hidden_one_b[...], late.cross_grad_b[...]),
    )
    shipping.send_chip(0)
    put_matrix(packs, 16, PER_SIDE, tn(late.memory[...], outs.key_low[...]))
    shipping.send_chip(1)
    put_matrix(packs, 32, PER_SIDE, tn(late.memory[...], outs.value_low[...]))
    shipping.send_chip(2)
    put_matrix(
        packs, 48, PER_SIDE,
        tn(context[...], branch[...])
        + tn(late.cross_context_b[...], late.cross_branch_b[...]),
    )
    shipping.send_chip(3)
    stores.finish()
    shipping.finish()


class SelfFirst(NamedTuple):
    self_branch: Any = LOW_SQ
    weight_out: Any = MATRIX
    inverse_self: Any = PER_HEAD
    context: Any = LOW_SQ
    keys: Any = LOW_SQ
    values: Any = LOW_SQ
    queries: Any = LOW_SQ


class SelfThen(NamedTuple):
    context_b: Any = LOW_SQ
    self_branch_b: Any = LOW_SQ
    tokens: Any = LOW_SQ
    inputs_b: Any = LOW_SQ
    query_grad_b: Any = LOW_SQ
    key_grad_b: Any = LOW_SQ
    value_grad_b: Any = LOW_SQ


class SelfOuts(NamedTuple):
    query_grad: Any = LOW_SQ
    key_grad: Any = LOW_SQ
    value_grad: Any = LOW_SQ


class SelfWork(NamedTuple):
    probs: Any = PROBS
    grad_context: Any = LOW_SQ
    inner_rows: Any = INNER
    packs: Any = PACKS8
    flat: Any = FLAT


def self_back_kernel(direct, device, lengths, gain_sum, order, also, *refs):
    first_in, probs_in, then_in, targets, grad_outs, first, then, outs, work, sems = split(
        refs, SelfFirst(), 1, SelfThen(), SelfOuts(), 2 if direct else 1, SelfFirst(),
        SelfThen(), SelfOuts(), SelfWork(), 5,
    )
    first_sem, then_sem, probs_sem, out_sem, ship_sem = sems
    stores = Stores(SelfOuts._fields, outs, targets, out_sem)
    loads = Loads(
        SelfFirst._fields, first_in._replace(weight_out=one_matrix(first_in.weight_out, 3)),
        first, first_sem,
    ).start()
    late = Loads(SelfThen._fields, then_in, then, then_sem)
    copies = PairCopies(probs_in[0], work.probs, probs_sem, late)
    branch = loads.self_branch
    weight = matrix(loads.weight_out, 0, PER_SIDE)
    inverse, context = loads.inverse_self, loads.context
    attend_backward(
        total_of(lengths), WINDOWS_SELF, loads.queries, loads.keys, loads.values, work.probs,
        inverse, context, lambda rows: nt(branch[rows], weight), work.grad_context,
        work.inner_rows, outs.query_grad, putter(outs.key_grad), putter(outs.value_grad), copies,
    )
    stores.start(*SelfOuts._fields)
    packs = work.packs
    shipping = Shipping(direct, device, packs, grad_outs, ship_sem)
    if direct:
        pack_norms(gain_sum, work.flat, packs, 0, 8)
    put_matrix(
        packs, 48, PER_SIDE,
        tn(context[...], branch[...]) + tn(late.context_b[...], late.self_branch_b[...]),
    )
    shipping.send_chip(3)
    pairs = (
        (outs.query_grad, late.query_grad_b),
        (outs.key_grad, late.key_grad_b),
        (outs.value_grad, late.value_grad_b),
    )
    for which, (grad, grad_b) in enumerate(pairs):
        put_matrix(
            packs, which * 16, PER_SIDE,
            tn(late.tokens[...], grad[...]) + tn(late.inputs_b[...], grad_b[...]),
        )
        shipping.send_chip(which)
    stores.finish()
    shipping.finish()


class InputGrads(NamedTuple):
    key_low: Any = LOW_SQ
    value_low: Any = LOW_SQ
    wall_cross: Any = ((32 * BLK, BLK), LOW)
    grad_first: Any = F32_SQ
    query_grad: Any = LOW_SQ
    key_grad: Any = LOW_SQ
    value_grad: Any = LOW_SQ
    wall_self: Any = ((48 * BLK, BLK), LOW)


def input_grads_kernel(order, *refs):
    size = len(InputGrads._fields)
    sources, refs = InputGrads(*refs[:size]), refs[size:]
    token_grad, memory_grad = refs[:2]
    targets, sems = refs[2 : 2 + size], refs[2 + size]
    sources = sources._replace(
        wall_cross=sources.wall_cross.at[pl.ds(16 * BLK, 32 * BLK)],
        wall_self=sources.wall_self.at[pl.ds(0, 48 * BLK)],
    )
    loads = Loads(InputGrads._fields, sources, targets, sems).start()
    key_low, value_low, wall = loads.key_low, loads.value_low, loads.wall_cross
    weights = [attn_matrix(wall, which) for which in range(2)]
    for rows in chunks():
        memory_grad[rows] = nt(key_low[rows], weights[0]) + nt(value_low[rows], weights[1])
    grad_first, query_grad, key_grad = loads.grad_first, loads.query_grad, loads.key_grad
    value_grad, wall = loads.value_grad, loads.wall_self
    weights = [attn_matrix(wall, which) for which in range(3)]
    for rows in chunks():
        token_grad[rows] = (
            grad_first[rows]
            + nt(query_grad[rows], weights[0])
            + nt(key_grad[rows], weights[1])
            + nt(value_grad[rows], weights[2])
        )


def shampoo_kernel(grad, weights, graft, left_stat, right_stat, left_root, right_root,
                   new_blocks, new_graft, new_left, new_right):
    for block in range(grad.shape[0]):
        values = grad[block]
        low = values.astype(LOW)
        new_left[block] = STAT_DECAY * left_stat[block] + (1.0 - STAT_DECAY) * nt(low, low)
        new_right[block] = STAT_DECAY * right_stat[block] + (1.0 - STAT_DECAY) * tn(low, low)
        moment = STAT_DECAY * graft[block] + (1.0 - STAT_DECAY) * values * values
        new_graft[block] = moment
        half_way = nn(left_root[block].astype(LOW), low)
        direction = nn(half_way.astype(LOW), right_root[block].astype(LOW))
        adaptive = values / (jnp.sqrt(moment) + GRAFT_EPS)
        ratio = jnp.sqrt(jnp.mean(adaptive * adaptive, keepdims=True)) * lax.rsqrt(
            jnp.mean(direction * direction, keepdims=True) + RATIO_EPS
        )
        new_blocks[block] = weights[block] - BLOCK_RATE * ratio * direction


def shapes_of(*tables):
    return [jax.ShapeDtypeStruct(shape, dtype) for table in tables for shape, dtype in table]


def scratch_of(*tables):
    return [VM(shape, dtype) for table in tables for shape, dtype in table]


def call(kernel, ins, outs, scratch, vmem, busy):
    return pl.pallas_call(
        kernel,
        out_shape=[shape for _, shape in outs],
        in_specs=[pl.BlockSpec(memory_space=space) for space, _ in ins],
        out_specs=[pl.BlockSpec(memory_space=space) for space, _ in outs],
        scratch_shapes=scratch,
        compiler_params=pltpu.CompilerParams(vmem_limit_bytes=vmem),
        cost_estimate=pl.CostEstimate(
            flops=busy * 1_000_000_000 + 1000, bytes_accessed=1000, transcendentals=0
        ),
    )(*[array for _, array in ins])


def inside(space, tables):
    return [(space, shape) for shape in shapes_of(tables)]


class Routes:
    def __init__(self, sides):
        self.sides = sides
        self.places = [
            (z, y, x, core)
            for z in range(sides[0])
            for y in range(sides[1])
            for x in range(sides[2])
            for core in range(2)
        ]

    def index(self, place):
        z, y, x, core = place
        return ((z * self.sides[1] + y) * self.sides[2] + x) * 2 + core

    def move(self, values, step):
        pairs = []
        for place in self.places:
            target = step(*place)
            if target is not None:
                pairs.append((self.index(place), self.index(target)))
        return lax.ppermute(values, AXES, pairs)


def to_core(z, y, x, core):
    return (z, y, x, 1 - core)


def to_x(z, y, x, core):
    return (z, y, 1 - x, core)


def to_y(z, y, x, core):
    return (z, 1 - y, x, core)


def hop_one(z, y, x, core):
    return to_y(z, y, x, core) if core == 0 else to_x(z, y, x, core)


def hop_two(z, y, x, core):
    return to_x(z, y, x, core) if core == 0 else to_y(z, y, x, core)


def ring_z(z, y, x, core):
    return ((z + 1) % 4, y, x, core)


def swap_z(z, y, x, core):
    return (z ^ 1, y, x, core)


def z_onto_high(z, y, x, core):
    return (z + 2, y, x, core) if z < 2 else None


def gather_pieces(routes, packed):
    along = [packed]
    for _ in range(3):
        along.append(routes.move(along[-1], ring_z))
    pieces = []
    for piece in along:
        first = routes.move(piece, hop_one)
        second = routes.move(piece, hop_two)
        third = routes.move(first, hop_two)
        for values in (piece, first, second, third):
            pieces += [values, routes.move(values, to_core)]
    return pieces


PACK = ((PACK_ROWS, BLK), LOW)


def sum_kernel(jobs, term_count, out_count, device, *refs):
    terms, outs = refs[:term_count], refs[-out_count - 4 : -4]
    parts, sums, sems, out_sems = refs[-4:]
    loads, number = [], 0
    for job in jobs:
        mine = []
        for term, slot, group in job:
            source = terms[term].at[slot, group]
            mine.append(pltpu.make_async_copy(source, parts.at[number], sems.at[number]))
            mine[-1].start()
            number += 1
        loads.append(mine)
    number = 0
    copies = []
    for place, mine in enumerate(loads):
        total = None
        for load in mine:
            load.wait()
            part = parts[number].astype(F32)
            total = part if total is None else total + part
            number += 1
        sums[place] = total.astype(LOW)
        if out_count == 1:
            copies.append(
                pltpu.make_async_copy(sums.at[place], outs[0].at[place], out_sems.at[place])
            )
            copies[-1].start()
    if out_count == 2:
        odd = place_of(device)[0] & 1
        for place in range(2):
            source = sums.at[odd if place else 1 - odd]
            copies.append(pltpu.make_async_copy(source, outs[place].at[0], out_sems.at[place]))
            copies[-1].start()
    for copy in copies:
        copy.wait()


def sum_packs(device, jobs, terms, after=(), sort=False, busy=3):
    count = sum(len(job) for job in jobs)
    shapes = [(1, PACK_ROWS, BLK)] * 2 if sort else [(len(jobs), PACK_ROWS, BLK)]
    return call(
        functools.partial(sum_kernel, jobs, len(terms), len(shapes)),
        [(pltpu.SMEM, device)] + [(pl.ANY, term) for term in (*terms, *after)],
        [(pl.ANY, jax.ShapeDtypeStruct(shape, LOW)) for shape in shapes],
        [VM((count, PACK_ROWS, BLK), LOW), VM((len(jobs), PACK_ROWS, BLK), LOW),
         pltpu.SemaphoreType.DMA((count,)), pltpu.SemaphoreType.DMA((len(jobs),))],
        PART_VMEM,
        busy,
    )


def far_sum(device, terms, groups, after=()):
    jobs = [[(0, slot, group), (1, slot, group)] for slot in (2, 3) for group in range(groups)]
    (away,) = sum_packs(device, jobs, terms, after)
    return away.reshape(2, groups, PACK_ROWS, BLK)


def near_job(first, group):
    return [(first, 1, group), (first + 1, 1, group), (first + 2, 1, group)]


def plane_job(first, group, last, place):
    own = [(first + term, 0, group) for term in range(3)]
    return own + [(last, 0, place)]


def over_z(routes, device, away, keep, near_step, far_step):
    near = routes.move(away, near_step)
    (away,) = sum_packs(device, [[(0, 0, 0), (1, 0, 0)]], [keep[None], near[None]])
    return [keep, near, routes.move(away, far_step)]


def over_plane(routes, device, terms, plane):
    def near(z, y, x, core):
        return (z ^ 1, y, x, core) if z % 2 != plane else None

    def far(z, y, x, core):
        return (plane, y, x, core) if z == plane + 2 else None

    (away,) = sum_packs(device, [near_job(0, 0)], terms)
    terms = terms + [routes.move(away, hop_one)[None]]
    (total,) = sum_packs(device, [plane_job(0, 0, 3, 0)], terms)
    return over_z(routes, device, total, total, near, far)


def shards(
    sides,
    tokens,
    memory,
    cotangent,
    lengths,
    blocks,
    norm_params,
    graft_state,
    left_stat,
    right_stat,
    left_root,
    right_root,
    norm_graft,
):
    direct = sides is not None
    blocks_low = blocks.astype(LOW).reshape(-1, BLK)
    norms_low = norm_params.astype(LOW)
    gains_in = []
    if direct:
        routes = Routes(sides)
        norm_rows = jnp.pad(norms_low[None], ((0, 15), (0, BLK - OWN_NORMS)))
        pieces = gather_pieces(routes, jnp.concatenate([blocks_low, norm_rows], axis=0))
    else:
        gains = lax.all_gather(norms_low, AXES, axis=0, tiled=True)
        gains_in = [jnp.pad(gains.astype(F32).reshape(6, D), ((0, 2), (0, 0)))]
        pieces = [lax.all_gather(blocks_low, AXES, axis=0, tiled=True)]

    device = lax.axis_index(AXES).astype(jnp.int32).reshape(1)
    smem, vmem, far = pltpu.SMEM, VM, pl.ANY
    square = jax.ShapeDtypeStruct((TOK_DEV, D), F32)
    square_low = jax.ShapeDtypeStruct((TOK_DEV, D), LOW)
    small = jax.ShapeDtypeStruct((8, D), F32)
    dma = pltpu.SemaphoreType.DMA
    ships = 2 if direct else 1

    def shipped(groups):
        return [(far, shape) for shape in grad_shapes(direct, groups)]

    def far_ins(table, found):
        return [(far, found[name]) for name in table._fields]

    outs = call(
        functools.partial(layers_kernel, direct, len(pieces)),
        [(smem, device), (smem, lengths), (far, tokens), (far, memory), (far, cotangent)]
        + [(vmem, gains) for gains in gains_in]
        + [(far, piece) for piece in pieces],
        [(vmem, square_low), (vmem, small), (vmem, small)] + shipped(2) + inside(far, Saved()),
        scratch_of(Held(), BothApps(), PerApp(), PerApp(), Branches())
        + [dma((2 * len(pieces),)), dma((3,)), dma((len(Saved()),)), dma((16,))],
        MAIN_VMEM,
        50,
    )
    decoded, gains, gain_sum = outs[:3]
    grads_mix = outs[3 : 3 + ships]
    found = dict(zip(Saved._fields, outs[3 + ships :]))
    found.update(memory=memory, tokens=tokens)

    order = [device]
    if direct:
        mix = [grads_mix[0], routes.move(grads_mix[1], to_core)]
        order = [far_sum(device, mix, 2)]
        mix.append(routes.move(order[0], hop_two))
    found.update(weight_out=found["wall_cross"], weight_query=found["wall_cross"])
    outs = call(
        functools.partial(cross_back_kernel, direct),
        [(smem, device), (smem, lengths), (vmem, gains), (vmem, gain_sum), (far, order[0])]
        + far_ins(CrossFirst, found) + [(far, found["probs_cross"])]
        + far_ins(CrossThen, found),
        inside(far, CrossOuts()) + shipped(1),
        scratch_of(CrossFirst(), CrossThen(), CrossOuts(), CrossWork())
        + [dma((len(CrossFirst()),)), dma((len(CrossThen()),)), dma((PAIRS,)),
           dma((len(CrossOuts()),)), dma((8,))],
        PART_VMEM,
        11,
    )
    found.update(zip(CrossOuts._fields, outs))
    grads_cross = outs[len(CrossOuts()) :]

    order = [device] * 2
    if direct:
        cross = [grads_cross[0], routes.move(grads_cross[1], to_core)]
        order = [
            sum_packs(device, [near_job(0, group) for group in range(2)], mix, busy=30)[0]
        ]
        order.append(far_sum(device, cross, 1, order))
        mix.append(routes.move(order[0], hop_one)[None])
        cross.append(routes.move(order[1], hop_two))
    found.update(weight_out=found["wall_self"])
    outs = call(
        functools.partial(self_back_kernel, direct),
        [(smem, device), (smem, lengths), (vmem, found["gain_sum"]), (far, order[0]),
         (far, order[1])]
        + far_ins(SelfFirst, found) + [(far, found["probs_self"])]
        + far_ins(SelfThen, found),
        inside(far, SelfOuts()) + shipped(1),
        scratch_of(SelfFirst(), SelfThen(), SelfOuts(), SelfWork())
        + [dma((len(SelfFirst()),)), dma((len(SelfThen()),)), dma((PAIRS,)),
           dma((len(SelfOuts()),)), dma((8,))],
        PART_VMEM,
        10,
    )
    found.update(zip(SelfOuts._fields, outs))
    grads_self = outs[len(SelfOuts()) :]

    order = device
    if direct:
        own = [grads_self[0], routes.move(grads_self[1], to_core)]
        mix_sums = sum_packs(
            device, [plane_job(0, 0, 3, 0), plane_job(0, 1, 3, 1)], mix, [cross[2]], True, 30
        )
        order = far_sum(device, own, 1, mix_sums)
        own.append(routes.move(order, hop_two))
    token_grad, memory_grad = call(
        input_grads_kernel,
        [(far, order)] + far_ins(InputGrads, found),
        [(vmem, square)] * 2,
        scratch_of(InputGrads()) + [dma((len(InputGrads()),))],
        PART_VMEM,
        5,
    )

    if direct:
        sums = [
            over_plane(routes, device, own, 0),
            over_plane(routes, device, cross, 1),
            over_z(routes, device, *mix_sums, swap_z, z_onto_high),
        ]
        own_sum, cross_sum, mix_sum = [
            sum(part[0].astype(F32) for part in parts) for parts in sums
        ]
        z = device[0] // (OWNERS // sides[0])
        pack = jnp.where(z >= 2, mix_sum, jnp.where(z == 1, cross_sum, own_sum))
        block_grad = pack[:OWN_ROWS].reshape(blocks.shape)
        norm_grad = pack[OWN_ROWS, :OWN_NORMS]
    else:
        terms = jnp.concatenate([grads_self[0], grads_cross[0], grads_mix[0]], axis=0)
        terms = terms.reshape(OWNERS, PACK_ROWS, BLK)[:, :OWN_ROWS].reshape(-1, BLK, BLK)
        block_grad = lax.psum_scatter(
            terms.astype(F32), AXES, scatter_dimension=0, tiled=True
        )
        norm_grad = lax.psum_scatter(
            found["gain_sum"][:6].reshape(-1), AXES, scatter_dimension=0, tiled=True
        )

    updates = (block_grad, blocks, graft_state, left_stat, right_stat, left_root, right_root)
    stack = jax.ShapeDtypeStruct(blocks.shape, F32)
    new_blocks, new_graft, new_left, new_right = call(
        shampoo_kernel, [(vmem, array) for array in updates], [(vmem, stack)] * 4, [],
        14 * 2**20, 5,
    )
    norm_moment = STAT_DECAY * norm_graft + (1.0 - STAT_DECAY) * norm_grad * norm_grad
    new_norms = norm_params - NORM_RATE * norm_grad / (jnp.sqrt(norm_moment) + GRAFT_EPS)
    return (
        decoded,
        token_grad,
        memory_grad,
        block_grad,
        new_blocks,
        new_graft,
        new_left,
        new_right,
        norm_grad,
        new_norms,
        norm_moment,
    )


def solution(mesh):
    rows = P(AXES, None)
    stack = P(AXES, None, None)
    flat = P(AXES)
    sides = GRIDS.get(mesh.shape["dp"]) if mesh.shape["rep"] == 2 else None
    return jax.shard_map(
        functools.partial(shards, sides),
        mesh=mesh,
        in_specs=(rows, rows, rows, rows, stack, flat, stack, stack, stack, stack, stack, flat),
        out_specs=(rows, rows, rows, stack, stack, stack, stack, stack, flat, flat, flat),
        check_vma=False,
    )
```

```python
import functools
from typing import Any, NamedTuple

import jax
import jax.numpy as jnp
from jax import lax
from jax.experimental import pallas as pl
from jax.experimental.pallas import tpu as pltpu
from jax.sharding import PartitionSpec as P

D = 512
HEADS = 8
FF = 2048
BLK = 128
TOK_DEV = 512
PER_SIDE = D // BLK
PANELS = FF // D
PAIRS = HEADS // 2
HALF = 256

STAT_DECAY = 0.5
BLOCK_RATE = 0.05
NORM_RATE = 0.2
NORM_EPS = 1e-05
GRAFT_EPS = 1e-08
RATIO_EPS = 1e-06
MASKED = -1e30
SCALE = (D // HEADS) ** (-0.5)

AXES = ("dp", "rep")
F32 = jnp.float32
LOW = jnp.bfloat16
MAIN_VMEM = 60 * 2**20
PART_VMEM = 63 * 2**20 + 2**19
SMALL_VMEM = 16 * 2**20

GRIDS = {16: (4, 2, 2)}

OWNERS = 32
OWN_BLOCKS = 8
OWN_NORMS = 96
OWN_ROWS = OWN_BLOCKS * BLK
PACK_ROWS = OWN_ROWS + 16

VM = pltpu.VMEM
WINDOWS_SELF = ((0, 256), (128, 384))
WINDOWS_CROSS = ((0, 512), (128, 384))
WINDOWS_ALL = ((0, 512), (0, 512))


def dot(left_mat, right_mat, left_dim, right_dim):
    return lax.dot_general(
        left_mat,
        right_mat,
        (((left_dim,), (right_dim,)), ((), ())),
        preferred_element_type=F32,
    )


def nn(left_mat, right_mat):
    return dot(left_mat, right_mat, 1, 0)


def nt(left_mat, right_mat):
    return dot(left_mat, right_mat, 1, 1)


def tn(left_mat, right_mat):
    return dot(left_mat, right_mat, 0, 0)


def matrix(wall, base, stride):
    def block(number):
        return wall[number * BLK : (number + 1) * BLK]

    rows = [
        jnp.concatenate([block(base + i * stride + j) for j in range(PER_SIDE)], axis=1)
        for i in range(PER_SIDE)
    ]
    return jnp.concatenate(rows, axis=0)


def attn_matrix(wall, which):
    return matrix(wall, which * PER_SIDE * PER_SIDE, PER_SIDE)


def up_panel(wall, panel):
    return matrix(wall, 128 + panel * PER_SIDE, FF // BLK)


def down_panel(wall, panel):
    return matrix(wall, 192 + panel * PER_SIDE * PER_SIDE, PER_SIDE)


def put_matrix(packs, base, stride, values):
    values = values.astype(packs.dtype)
    for i in range(PER_SIDE):
        for j in range(PER_SIDE):
            owner, place = divmod(base + i * stride + j, OWN_BLOCKS)
            first = owner * PACK_ROWS + place * BLK
            packs[first : first + BLK] = values[i * BLK : (i + 1) * BLK, j * BLK : (j + 1) * BLK]


def lanes_below(count, rows=1):
    return lax.broadcasted_iota(jnp.int32, (rows, BLK), 1) < count


def unpack_norms(packed, gains):
    turned = {shift: pltpu.roll(packed, shift, 1) for shift in (32, 64, 96)}
    turned[0] = packed
    for row in range(6 * D // BLK):
        owner, offset = divmod(row * BLK, OWN_NORMS)
        kept = OWN_NORMS - offset
        values = jnp.where(
            lanes_below(kept),
            turned[-offset % BLK][owner : owner + 1],
            turned[kept][owner + 1 : owner + 2],
        )
        gains[row // 4 : row // 4 + 1, (row % 4) * BLK : (row % 4 + 1) * BLK] = values


def pack_norms(gain_sum, flat, packs, first_owner, owners):
    for row in range(6 * D // BLK):
        flat[row : row + 1] = gain_sum[
            row // 4 : row // 4 + 1, (row % 4) * BLK : (row % 4 + 1) * BLK
        ]
    flat[24:32] = jnp.zeros((8, BLK), F32)
    values = flat[...]
    turned = {shift: pltpu.roll(values, shift, 1) for shift in (32, 64, 96)}
    turned[0] = values
    top = lax.broadcasted_iota(jnp.int32, (16, BLK), 0) == 0
    for owner in range(owners):
        row, offset = divmod((first_owner + owner) * OWN_NORMS, BLK)
        source = turned[-offset % BLK]
        mine = jnp.where(
            lanes_below(BLK - offset), source[row : row + 1], source[row + 1 : row + 2]
        )
        last = owner * PACK_ROWS + OWN_ROWS
        packs[last : last + 16] = jnp.where(top, mine, 0.0).astype(packs.dtype)


def norm_forward(values, gain, bias):
    center = values - jnp.mean(values, axis=1, keepdims=True)
    spread = jnp.mean(center * center, axis=1, keepdims=True)
    scale = lax.rsqrt(spread + NORM_EPS)
    unit = center * scale
    return unit * gain + bias, unit, scale


def norm_backward(grad, unit, scale, gain):
    inner = grad * gain
    first = jnp.mean(inner, axis=1, keepdims=True)
    second = jnp.mean(inner * unit, axis=1, keepdims=True)
    grad_in = (inner - first - unit * second) * scale
    grad_gain = jnp.sum(grad * unit, axis=0, keepdims=True)
    grad_bias = jnp.sum(grad, axis=0, keepdims=True)
    return grad_in, grad_gain, grad_bias


def chunks():
    return [pl.ds(start, HALF) for start in range(0, TOK_DEV, HALF)]


def pick_half(values, side):
    lane = lax.broadcasted_iota(jnp.int32, values.shape, 1)
    mine = lane < D // HEADS if side == 0 else lane >= D // HEADS
    return jnp.where(mine, values, jnp.zeros_like(values))


def both_halves(values, axis=0):
    return jnp.concatenate([pick_half(values, 0), pick_half(values, 1)], axis=axis)


def heads_wide(narrow):
    head_of = lax.broadcasted_iota(jnp.int32, (BLK, D), 1) // (D // HEADS)
    chooser = (head_of == lax.broadcasted_iota(jnp.int32, (BLK, D), 0)).astype(F32).astype(LOW)
    high = narrow.astype(LOW)
    rest = (narrow - high.astype(F32)).astype(LOW)
    return nn(
        jnp.concatenate([high, rest], axis=1), jnp.concatenate([chooser, chooser], axis=0)
    )


def for_pairs(total, windows, pair_step, copies=None):
    @pl.when(total >= BLK)
    def _():
        for pair in range(PAIRS):
            if copies is not None:
                copies.wait(pair)
            pair_step(windows, pair, pl.ds(pair * BLK, BLK))

    @pl.when(total < BLK)
    def _():
        if copies is not None:
            for pair in range(PAIRS):
                copies.wait(pair)

        def step(pair, carry):
            pair_step(WINDOWS_ALL, pair, pl.ds(pl.multiple_of(pair * BLK, BLK), BLK))
            return carry

        lax.fori_loop(0, PAIRS, step, 0)


def attend_forward(
    total, windows, queries, key_rows, value_rows, bias, probs, raw, inverse, context
):
    inverse[...] = jnp.zeros_like(inverse)

    def pair_step(spans, pair, lanes):
        for part, (start, size) in enumerate(spans):
            rows = pl.ds(part * HALF, HALF)
            span = pl.ds(start, size)
            query = queries[rows, lanes]
            keys = key_rows[span, lanes]
            values = value_rows[span, lanes]
            lane = lax.broadcasted_iota(jnp.int32, (size, BLK), 1)
            scores = [nt(keys, pick_half(query, side)) for side in range(2)]
            weights, sources = [], []
            for side in range(2):
                masked = scores[side] + bias[span, rows]
                top = jnp.max(masked, axis=0, keepdims=True)
                weight = jnp.exp(masked - top).astype(LOW)
                probs[2 * pair + side, span, rows] = weight
                weights.append(weight)
                ones = (lane == 2 * pair + side).astype(F32).astype(LOW)
                sources.append(jnp.concatenate([pick_half(values, side), ones], axis=1))
            mixed = tn(jnp.concatenate(weights, axis=0), jnp.concatenate(sources, axis=0))
            raw[rows, lanes] = mixed[:, :BLK]
            inverse[rows] += mixed[:, BLK:]

    for_pairs(total, windows, pair_step)
    for rows in chunks():
        sums = inverse[rows]
        narrow = jnp.where(sums > 0.0, 1.0 / sums, 0.0)
        inverse[rows] = narrow
        context[rows] = (raw[rows] * heads_wide(narrow)).astype(LOW)


def attend_backward(
    total, windows, queries, key_rows, value_rows, probs, inverse, context, grad_of,
    grad_context, inner_rows, grad_queries, put_keys, put_values, copies=None,
):
    head_of = lax.broadcasted_iota(jnp.int32, (16, D), 1) // (D // HEADS)
    chooser = (head_of == lax.broadcasted_iota(jnp.int32, (16, D), 0)).astype(F32).astype(LOW)
    for rows in chunks():
        grad = (grad_of(rows) * heads_wide(inverse[rows])).astype(LOW)
        grad_context[rows] = grad
        inner = grad.astype(F32) * context[rows].astype(F32)
        high = inner.astype(LOW)
        rest = (inner - high.astype(F32)).astype(LOW)
        inner_rows[:, rows] = nt(chooser, high) + nt(chooser, rest)

    def pair_step(spans, pair, lanes):
        shares = []
        for part, (start, size) in enumerate(spans):
            rows = pl.ds(part * HALF, HALF)
            span = pl.ds(start, size)
            keys = key_rows[span, lanes]
            values = value_rows[span, lanes]
            grad = grad_context[rows, lanes]
            weights = [probs[2 * pair + side, span, rows] for side in range(2)]
            grad_probs = [nt(values, pick_half(grad, side)) for side in range(2)]
            slopes = []
            for side in range(2):
                base = inner_rows[pl.ds(2 * pair + side, 1), rows]
                slopes.append((weights[side].astype(F32) * (grad_probs[side] - base)).astype(LOW))
            grad_queries[rows, lanes] = (
                tn(jnp.concatenate(slopes, axis=0), both_halves(keys)) * SCALE
            ).astype(LOW)
            shares.append(
                (
                    nn(jnp.concatenate(slopes, axis=1), both_halves(queries[rows, lanes])),
                    nn(jnp.concatenate(weights, axis=1), both_halves(grad)),
                )
            )
        for first in range(0, TOK_DEV, BLK):
            rows = pl.ds(first, BLK)
            for which, put in enumerate((put_keys, put_values)):
                parts = [
                    share[which][first - start : first - start + BLK]
                    for share, (start, size) in zip(shares, spans)
                    if start <= first < start + size
                ]
                put(rows, lanes, sum(parts[1:], parts[0]))

    for_pairs(total, windows, pair_step, copies)


def putter(target):
    def put(rows, lanes, values):
        target[rows, lanes] = values.astype(target.dtype)

    return put


def total_of(lengths):
    total = lengths[0, 0]
    for number in range(1, lengths.shape[1]):
        total = total + lengths[0, number]
    return total


def place_of(device):
    number = device[0]
    return number >> 3, (number >> 2) & 1, (number >> 1) & 1, number & 1


def make_biases(lengths, bias_self, bias_cross):
    count = lengths.shape[1]
    row = lax.broadcasted_iota(jnp.int32, (32, 1), 0)
    low = jnp.zeros((32, 1), jnp.int32)
    high = jnp.zeros((32, 1), jnp.int32)
    bound = jnp.int32(0)
    for number in range(count):
        low = jnp.where(row == number, bound, low)
        bound = bound + lengths[0, number]
        high = jnp.where(row == number, bound, high)
    low = jnp.where(row == count, bound, low)
    high = jnp.where(row == count, TOK_DEV, high)
    slot = lax.broadcasted_iota(jnp.int32, (32, TOK_DEV), 1)
    member = ((slot >= low) & (slot < high)).astype(F32).astype(LOW)
    for rows in chunks():
        apart = (tn(member, member[:, rows.start : rows.start + HALF]) - 1.0) * -MASKED
        key = lax.broadcasted_iota(jnp.int32, apart.shape, 0)
        query = lax.broadcasted_iota(jnp.int32, apart.shape, 1) + rows.start
        bias_cross[:, rows] = apart
        bias_self[:, rows] = jnp.where(key <= query, apart, MASKED)


class Shipping:
    def __init__(self, direct, device, packs, outs, sems):
        self.direct, self.packs, self.outs, self.sems = direct, packs, outs, sems
        _, self.y, self.x, self.core = place_of(device)
        self.waits = []

    def send(self, group, chip, core):
        number = (group * 4 + chip) * 2 + core
        source = self.packs.at[pl.ds(number * PACK_ROWS, PACK_ROWS)]
        sem = self.sems.at[number]
        if not self.direct:
            target = self.outs[0].at[pl.ds(number * PACK_ROWS, PACK_ROWS)]
            self.waits.append(pltpu.make_async_copy(source, target, sem))
            self.waits[-1].start()
            return
        move_y, move_x = self.y ^ (chip >> 1), self.x ^ (chip & 1)
        slot = move_x * 2 + move_y if core == 0 else move_y * 2 + move_x
        keep = pltpu.make_async_copy(source, self.outs[0].at[slot, group], sem)
        side = slot & 1

        @pl.when(self.core == core)
        def _():
            keep.start()

        @pl.when((self.core != core) & (slot >= 2))
        def _():
            pltpu.make_async_copy(source, self.outs[1].at[side, group], sem).start()

        @pl.when((self.core != core) & (slot < 2))
        def _():
            pltpu.make_async_copy(source, self.outs[2].at[side, group], sem).start()

        self.waits.append(keep)

    def send_chip(self, chip):
        for core in range(2):
            self.send(0, chip, core)

    def finish(self):
        for copy in self.waits:
            copy.wait()


def grad_shapes(direct, groups):
    if direct:
        return [
            jax.ShapeDtypeStruct((slots, groups, PACK_ROWS, BLK), LOW) for slots in (4, 2, 2)
        ]
    return [jax.ShapeDtypeStruct((groups * 8 * PACK_ROWS, BLK), LOW)]


LOW_SQ = ((TOK_DEV, D), LOW)
F32_SQ = ((TOK_DEV, D), F32)
COLUMN = ((TOK_DEV, 1), F32)
PER_HEAD = ((TOK_DEV, BLK), F32)
PROBS = ((HEADS, TOK_DEV, TOK_DEV), LOW)
WALL64 = ((64 * BLK, BLK), LOW)
PACKS8 = ((8 * PACK_ROWS, BLK), LOW)
WIDE = ((TOK_DEV, FF), LOW)
GAINS = ((8, D), F32)
INNER = ((16, TOK_DEV), F32)
FLAT = ((32, BLK), F32)


class Saved(NamedTuple):
    wall_self: Any = WALL64
    wall_cross: Any = WALL64
    probs_self: Any = PROBS
    probs_cross: Any = PROBS
    inverse_self: Any = PER_HEAD
    inverse_cross: Any = PER_HEAD
    queries: Any = LOW_SQ
    keys: Any = LOW_SQ
    values: Any = LOW_SQ
    context: Any = LOW_SQ
    hidden_one: Any = LOW_SQ
    cross_queries: Any = LOW_SQ
    cross_context: Any = LOW_SQ
    unit_one: Any = F32_SQ
    scale_one: Any = COLUMN
    mem_keys: Any = LOW_SQ
    mem_values: Any = LOW_SQ
    grad_second: Any = F32_SQ
    cross_branch: Any = LOW_SQ
    inputs_b: Any = LOW_SQ
    context_b: Any = LOW_SQ
    hidden_one_b: Any = LOW_SQ
    cross_context_b: Any = LOW_SQ
    cross_branch_b: Any = LOW_SQ
    cross_grad_b: Any = LOW_SQ
    self_branch_b: Any = LOW_SQ
    query_grad_b: Any = LOW_SQ
    key_grad_b: Any = LOW_SQ
    value_grad_b: Any = LOW_SQ
    mem_key_grad_b: Any = F32_SQ
    mem_value_grad_b: Any = F32_SQ


class Held(NamedTuple):
    tokens: Any = LOW_SQ
    memory: Any = LOW_SQ
    cotangent: Any = LOW_SQ
    bias_self: Any = F32_SQ
    bias_cross: Any = F32_SQ
    wall: Any = ((256 * BLK, BLK), LOW)
    norms: Any = ((OWNERS, 16, BLK), LOW)
    flat: Any = FLAT
    probs_self: Any = PROBS
    probs_cross: Any = PROBS
    inverse_self: Any = PER_HEAD
    inverse_cross: Any = PER_HEAD
    mem_keys: Any = LOW_SQ
    mem_values: Any = LOW_SQ
    state: Any = F32_SQ
    hidden: Any = F32_SQ
    grad_context: Any = LOW_SQ
    inner_rows: Any = INNER
    key_sum: Any = F32_SQ
    value_sum: Any = F32_SQ
    grad_second: Any = F32_SQ


class BothApps(NamedTuple):
    inputs: Any = LOW_SQ
    queries: Any = LOW_SQ
    keys: Any = LOW_SQ
    values: Any = LOW_SQ
    context: Any = LOW_SQ
    unit_one: Any = F32_SQ
    scale_one: Any = COLUMN
    hidden_one: Any = LOW_SQ
    cross_queries: Any = LOW_SQ
    cross_context: Any = LOW_SQ


class PerApp(NamedTuple):
    unit_two: Any = F32_SQ
    scale_two: Any = COLUMN
    hidden_two: Any = LOW_SQ
    gelu_slope: Any = WIDE
    activated: Any = WIDE
    unit_three: Any = F32_SQ
    scale_three: Any = COLUMN
    down_branch: Any = LOW_SQ


class Branches(NamedTuple):
    cross_branch: Any = LOW_SQ
    cross_grad: Any = LOW_SQ
    self_branch: Any = LOW_SQ
    query_grad: Any = LOW_SQ
    key_grad: Any = LOW_SQ
    value_grad: Any = LOW_SQ


def gelu_parts(values):
    first = 0.7978845608028654
    cubic = 0.044715 * first
    square = values * values
    bend = jnp.tanh(values * (first + cubic * square))
    half = 0.5 + 0.5 * bend
    slope = half + (0.5 * values) * (1.0 - bend * bend) * (first + (3.0 * cubic) * square)
    return values * half, slope


def attend_self(app, held, bias, total):
    weights = [attn_matrix(held.wall, which) for which in range(3)]
    for rows in chunks():
        inputs = held.state[rows].astype(LOW)
        app.inputs[rows] = inputs
        app.queries[rows] = (nn(inputs, weights[0]) * SCALE).astype(LOW)
        app.keys[rows] = nn(inputs, weights[1]).astype(LOW)
        app.values[rows] = nn(inputs, weights[2]).astype(LOW)
    attend_forward(
        total, WINDOWS_SELF, app.queries, app.keys, app.values, bias, held.probs_self,
        held.hidden, held.inverse_self, app.context,
    )


def finish_self(app, held, gains):
    weight = attn_matrix(held.wall, 3)
    for rows in chunks():
        total_rows = held.state[rows] + nn(app.context[rows], weight)
        out, unit, scale = norm_forward(total_rows, gains[0:1], gains[1:2])
        app.unit_one[rows] = unit
        app.scale_one[rows] = scale
        app.hidden_one[rows] = out.astype(LOW)
        held.hidden[rows] = out


def forward_cross(app, held, gains, bias, total):
    weight = attn_matrix(held.wall, 4)
    for rows in chunks():
        app.cross_queries[rows] = (nn(app.hidden_one[rows], weight) * SCALE).astype(LOW)
    attend_forward(
        total, WINDOWS_CROSS, app.cross_queries, held.mem_keys, held.mem_values, bias,
        held.probs_cross, held.state, held.inverse_cross, app.cross_context,
    )
    weight = attn_matrix(held.wall, 7)
    for rows in chunks():
        total_rows = held.hidden[rows] + nn(app.cross_context[rows], weight)
        out, unit, scale = norm_forward(total_rows, gains[2:3], gains[3:4])
        app.unit_two[rows] = unit
        app.scale_two[rows] = scale
        app.hidden_two[rows] = out.astype(LOW)
        held.hidden[rows] = out


def forward_mix(app, held, gains, finish):
    for rows in chunks():
        mixed = app.hidden_two[rows]
        total_rows = held.hidden[rows]
        for panel in range(PANELS):
            lanes = pl.ds(panel * D, D)
            active, slope = gelu_parts(nn(mixed, up_panel(held.wall, panel)))
            active = active.astype(LOW)
            app.activated[rows, lanes] = active
            app.gelu_slope[rows, lanes] = slope.astype(LOW)
            total_rows = total_rows + nn(active, down_panel(held.wall, panel))
        out, unit, scale = norm_forward(total_rows, gains[4:5], gains[5:6])
        app.unit_three[rows] = unit
        app.scale_three[rows] = scale
        finish(rows, out)


def backward_mix(app, held, gains, gain_sum, grad_of, branch):
    for rows in chunks():
        grad_third, gain3, bias3 = norm_backward(
            grad_of(rows), app.unit_three[rows], app.scale_three[rows], gains[4:5]
        )
        gain_sum[4:5] += gain3
        gain_sum[5:6] += bias3
        grad_low = grad_third.astype(LOW)
        app.down_branch[rows] = grad_low
        for panel in range(PANELS):
            lanes = pl.ds(panel * D, D)
            grad_active = nt(grad_low, down_panel(held.wall, panel))
            grad_pre = (grad_active * app.gelu_slope[rows, lanes].astype(F32)).astype(LOW)
            app.gelu_slope[rows, lanes] = grad_pre
            grad_third = grad_third + nt(grad_pre, up_panel(held.wall, panel))
        grad_in, gain2, bias2 = norm_backward(
            grad_third, app.unit_two[rows], app.scale_two[rows], gains[2:3]
        )
        gain_sum[2:3] += gain2
        gain_sum[3:4] += bias2
        held.grad_second[rows] = grad_in
        branch[rows] = grad_in.astype(LOW)


def backward_cross_end(app, weight, gains, gain_sum, grad_second, cross_grad, grad_first,
                       self_branch):
    for rows in chunks():
        grad = grad_second[rows] + nt(cross_grad[rows], weight)
        grad_in, gain1, bias1 = norm_backward(
            grad, app.unit_one[rows], app.scale_one[rows], gains[0:1]
        )
        gain_sum[0:1] += gain1
        gain_sum[1:2] += bias1
        grad_first[rows] = grad_in
        self_branch[rows] = grad_in.astype(LOW)


def layers_kernel(direct, piece_count, *refs):
    refs = list(refs)

    def take(table):
        count = table if isinstance(table, int) else len(table)
        taken, refs[:count] = refs[:count], []
        return taken if isinstance(table, int) else type(table)(*taken)

    device, lengths, tokens, memory, cotangent = take(5)
    gains_in = [] if direct else take(1)
    pieces = take(piece_count)
    decoded, gains, gain_sum = take(3)
    grad_outs = take(3 if direct else 1)
    saved = take(Saved())
    held = take(Held())
    both = take(BothApps())
    app_a, app_b, branches = take(PerApp()), take(PerApp()), take(Branches())
    piece_sem, input_sem, save_sem, ship_sem = take(4)

    class App(NamedTuple):
        inputs: Any
        queries: Any
        keys: Any
        values: Any
        context: Any
        unit_one: Any
        scale_one: Any
        hidden_one: Any
        cross_queries: Any
        cross_context: Any
        unit_two: Any
        scale_two: Any
        hidden_two: Any
        gelu_slope: Any
        activated: Any
        unit_three: Any
        scale_three: Any
        down_branch: Any

    app_a, app_b = App(*both, *app_a), App(*both, *app_b)
    wall = held.wall
    total = total_of(lengths)
    inputs = [
        pltpu.make_async_copy(source, target, input_sem.at[number])
        for number, (source, target) in enumerate(
            ((tokens, held.tokens), (memory, held.memory), (cotangent, held.cotangent))
        )
    ]
    inputs[0].start()
    if direct:
        arrive = fetch_pieces(device, pieces, wall, held.norms, piece_sem)
    else:
        whole = pltpu.make_async_copy(pieces[0], wall, piece_sem.at[0])
        whole.start()

        def arrive(group):
            if group == 0:
                whole.wait()

    for load in inputs[1:]:
        load.start()
    bias_self, bias_cross = held.bias_self, held.bias_cross
    make_biases(lengths, bias_self, bias_cross)
    gain_sum[...] = jnp.zeros_like(gain_sum)
    inputs[0].wait()
    memory, cotangent = held.memory, held.cotangent
    for rows in chunks():
        held.state[rows] = held.tokens[rows].astype(F32)
    arrive(0)

    stores = {}

    def save(target, source):
        number = len(stores)
        stores[number] = pltpu.make_async_copy(source, target, save_sem.at[number])
        stores[number].start()
        return number

    def settle(numbers):
        for number in numbers:
            stores[number].wait()

    walls = [save(saved.wall_self, wall.at[pl.ds(0, 64 * BLK)])]
    later = []
    gains[6:8] = jnp.zeros((2, D), F32)

    real = {
        start: lax.broadcasted_iota(jnp.int32, (HALF, 1), 0) + start < total
        for start in range(0, TOK_DEV, HALF)
    }

    def keep_state(rows, out):
        held.state[rows] = out

    def keep_decoded(rows, out):
        decoded[rows] = jnp.where(real[rows.start], out, 0.0).astype(LOW)

    attend_self(app_a, held, bias_self, total)
    arrive(1)
    arrive(2)
    arrive(3)
    if direct:
        for owner in range(OWNERS):
            held.flat[owner : owner + 1] = held.norms[owner].astype(F32)[0:1]
        unpack_norms(held.flat[...], gains)
    else:
        gains[...] = gains_in[0][...]
    walls.append(save(saved.wall_cross, wall.at[pl.ds(64 * BLK, 64 * BLK)]))
    for load in inputs[1:]:
        load.wait()
    weights = [attn_matrix(wall, which) for which in (5, 6)]
    for rows in chunks():
        held.mem_keys[rows] = nn(memory[rows], weights[0]).astype(LOW)
        held.mem_values[rows] = nn(memory[rows], weights[1]).astype(LOW)
    later += [save(saved.mem_keys, held.mem_keys), save(saved.mem_values, held.mem_values)]
    finish_self(app_a, held, gains)
    first_saves = [
        save(saved.probs_self, held.probs_self),
        save(saved.inverse_self, held.inverse_self),
        save(saved.queries, app_a.queries),
        save(saved.keys, app_a.keys),
        save(saved.values, app_a.values),
        save(saved.context, app_a.context),
        save(saved.hidden_one, app_a.hidden_one),
        save(saved.unit_one, app_a.unit_one),
        save(saved.scale_one, app_a.scale_one),
    ]
    forward_cross(app_a, held, gains, bias_cross, total)
    second_saves = [
        save(saved.probs_cross, held.probs_cross),
        save(saved.inverse_cross, held.inverse_cross),
        save(saved.cross_queries, app_a.cross_queries),
        save(saved.cross_context, app_a.cross_context),
    ]
    forward_mix(app_a, held, gains, keep_state)
    settle(first_saves)
    attend_self(app_b, held, bias_self, total)
    finish_self(app_b, held, gains)
    settle(second_saves)
    forward_cross(app_b, held, gains, bias_cross, total)
    forward_mix(app_b, held, gains, keep_decoded)
    later += [
        save(saved.inputs_b, app_b.inputs),
        save(saved.context_b, app_b.context),
        save(saved.hidden_one_b, app_b.hidden_one),
        save(saved.cross_context_b, app_b.cross_context),
    ]

    def last_grad(rows):
        return jnp.where(real[rows.start], cotangent[rows].astype(F32), 0.0)

    backward_mix(app_b, held, gains, gain_sum, last_grad, branches.cross_branch)
    later.append(save(saved.cross_branch_b, branches.cross_branch))
    weight = attn_matrix(wall, 7)
    attend_backward(
        total, WINDOWS_CROSS, app_b.cross_queries, held.mem_keys, held.mem_values,
        held.probs_cross, held.inverse_cross, app_b.cross_context,
        lambda rows: nt(branches.cross_branch[rows], weight), held.grad_context,
        held.inner_rows, branches.cross_grad, putter(held.key_sum), putter(held.value_sum),
    )
    later += [
        save(saved.mem_key_grad_b, held.key_sum),
        save(saved.mem_value_grad_b, held.value_sum),
        save(saved.cross_grad_b, branches.cross_grad),
    ]
    backward_cross_end(
        app_b, attn_matrix(wall, 4), gains, gain_sum, held.grad_second, branches.cross_grad,
        held.hidden, branches.self_branch,
    )
    later.append(save(saved.self_branch_b, branches.self_branch))
    weight_out = attn_matrix(wall, 3)
    attend_backward(
        total, WINDOWS_SELF, app_b.queries, app_b.keys, app_b.values, held.probs_self,
        held.inverse_self, app_b.context,
        lambda rows: nt(branches.self_branch[rows], weight_out), held.grad_context,
        held.inner_rows, branches.query_grad, putter(branches.key_grad),
        putter(branches.value_grad),
    )
    later += [
        save(saved.query_grad_b, branches.query_grad),
        save(saved.key_grad_b, branches.key_grad),
        save(saved.value_grad_b, branches.value_grad),
    ]
    weights = [attn_matrix(wall, which) for which in range(3)]
    for rows in chunks():
        held.state[rows] = (
            held.hidden[rows]
            + nt(branches.query_grad[rows], weights[0])
            + nt(branches.key_grad[rows], weights[1])
            + nt(branches.value_grad[rows], weights[2])
        )
    backward_mix(
        app_a, held, gains, gain_sum, lambda rows: held.state[rows], held.grad_context
    )
    later += [
        save(saved.grad_second, held.grad_second),
        save(saved.cross_branch, held.grad_context),
    ]

    settle(walls)
    packs = wall
    if direct:
        pack_norms(gain_sum, held.flat, packs, 16, 16)
    shipping = Shipping(direct, device, packs, grad_outs, ship_sem)
    for panel in range(PANELS):
        lanes = pl.ds(panel * D, D)
        put_matrix(
            packs, panel * PER_SIDE, FF // BLK,
            tn(app_a.hidden_two[...], app_a.gelu_slope[:, lanes])
            + tn(app_b.hidden_two[...], app_b.gelu_slope[:, lanes]),
        )
        if panel % 2 == 1:
            for chip in range(4):
                shipping.send(0, chip, panel // 2)
    for panel in range(PANELS):
        lanes = pl.ds(panel * D, D)
        put_matrix(
            packs, 64 + panel * PER_SIDE * PER_SIDE, PER_SIDE,
            tn(app_a.activated[:, lanes], app_a.down_branch[...])
            + tn(app_b.activated[:, lanes], app_b.down_branch[...]),
        )
        for core in range(2):
            shipping.send(1, panel, core)
    settle(later)
    shipping.finish()


def fetch_pieces(device, pieces, wall, norms, sems):
    z, y, x, core = place_of(device)
    copies = []
    for number, piece in enumerate(pieces):
        back, spot, other = number >> 3, (number >> 1) & 3, number & 1
        one, two = spot & 1, spot >> 1
        lane = core ^ other
        at_y = y ^ jnp.where(lane == 0, one, two)
        at_x = x ^ jnp.where(lane == 0, two, one)
        owner = ((((z - back) & 3) * 2 + at_y) * 2 + at_x) * 2 + lane
        copies.append(
            (
                pltpu.make_async_copy(
                    piece.at[pl.ds(0, OWN_ROWS)],
                    wall.at[pl.ds(pl.multiple_of(owner * OWN_ROWS, OWN_ROWS), OWN_ROWS)],
                    sems.at[2 * number],
                ),
                pltpu.make_async_copy(
                    piece.at[pl.ds(OWN_ROWS, 16)], norms.at[owner], sems.at[2 * number + 1]
                ),
            )
        )
    def for_plane(plane, act):
        for back in range(4):

            @pl.when(((z - plane) & 3) == back)
            def _(back=back):
                for pair in copies[back * 8 : back * 8 + 8]:
                    for copy in pair:
                        act(copy)

    def arrive(plane):
        for_plane(plane, lambda copy: copy.wait())
        if plane == 0:
            for other in range(1, 4):
                for_plane(other, lambda copy: copy.start())

    for_plane(0, lambda copy: copy.start())
    return arrive


class Loads:
    def __init__(self, names, sources, targets, sems):
        self.targets = dict(zip(names, targets))
        self.copies = {
            name: pltpu.make_async_copy(source, target, sems.at[number])
            for number, (name, source, target) in enumerate(zip(names, sources, targets))
        }

    def start(self):
        for copy in self.copies.values():
            copy.start()
        return self

    def __getattr__(self, name):
        if name in self.copies:
            self.copies.pop(name).wait()
        return self.targets[name]


class Stores:
    def __init__(self, names, sources, targets, sems):
        self.copies = {
            name: pltpu.make_async_copy(source, target, sems.at[number])
            for number, (name, source, target) in enumerate(zip(names, sources, targets))
        }

    def start(self, *names):
        for name in names:
            self.copies[name].start()

    def finish(self):
        for copy in self.copies.values():
            copy.wait()


def one_matrix(wall, which):
    return wall.at[pl.ds(which * 16 * BLK, 16 * BLK)]


class PairCopies:
    def __init__(self, source, target, sems, then):
        self.copies = [
            pltpu.make_async_copy(
                source.at[pl.ds(2 * pair, 2)], target.at[pl.ds(2 * pair, 2)], sems.at[pair]
            )
            for pair in range(PAIRS)
        ]
        self.copies[0].start()
        self.then = then

    def wait(self, pair):
        if pair == 0:
            for copy in self.copies[1:]:
                copy.start()
        self.copies[pair].wait()
        if pair == 1:
            self.then.start()


MATRIX = ((16 * BLK, BLK), LOW)


class CrossFirst(NamedTuple):
    cross_branch: Any = LOW_SQ
    weight_out: Any = MATRIX
    inverse_cross: Any = PER_HEAD
    cross_context: Any = LOW_SQ
    mem_keys: Any = LOW_SQ
    mem_values: Any = LOW_SQ
    cross_queries: Any = LOW_SQ


class CrossThen(NamedTuple):
    mem_key_grad_b: Any = F32_SQ
    mem_value_grad_b: Any = F32_SQ
    weight_query: Any = MATRIX
    grad_second: Any = F32_SQ
    unit_one: Any = F32_SQ
    scale_one: Any = COLUMN
    hidden_one: Any = LOW_SQ
    hidden_one_b: Any = LOW_SQ
    cross_grad_b: Any = LOW_SQ
    memory: Any = LOW_SQ
    cross_context_b: Any = LOW_SQ
    cross_branch_b: Any = LOW_SQ


class CrossOuts(NamedTuple):
    grad_first: Any = F32_SQ
    self_branch: Any = LOW_SQ
    gain_sum: Any = GAINS
    key_low: Any = LOW_SQ
    value_low: Any = LOW_SQ


class CrossWork(NamedTuple):
    probs: Any = PROBS
    key_sum: Any = F32_SQ
    value_sum: Any = F32_SQ
    grad_context: Any = LOW_SQ
    inner_rows: Any = INNER
    cross_grad: Any = LOW_SQ
    packs: Any = PACKS8
    flat: Any = FLAT


def split(refs, *parts):
    found, first = [], 0
    for part in parts:
        count = part if isinstance(part, int) else len(part)
        taken = refs[first : first + count]
        found.append(taken if isinstance(part, int) else type(part)(*taken))
        first += count
    return found


def cross_back_kernel(direct, device, lengths, gains, gain_before, order, *refs):
    first_in, probs_in, then_in, targets, grad_outs, first, then, outs, work, sems = split(
        refs, CrossFirst(), 1, CrossThen(), CrossOuts(), 3 if direct else 1, CrossFirst(),
        CrossThen(), CrossOuts(), CrossWork(), 5,
    )
    first_sem, then_sem, probs_sem, out_sem, ship_sem = sems
    stores = Stores(CrossOuts._fields, outs, targets, out_sem)
    loads = Loads(
        CrossFirst._fields, first_in._replace(weight_out=one_matrix(first_in.weight_out, 3)),
        first, first_sem,
    ).start()
    late = Loads(
        CrossThen._fields, then_in._replace(weight_query=one_matrix(then_in.weight_query, 0)),
        then, then_sem,
    )
    copies = PairCopies(probs_in[0], work.probs, probs_sem, late)
    outs.gain_sum[...] = gain_before[...]
    branch = loads.cross_branch
    weight = matrix(loads.weight_out, 0, PER_SIDE)
    inverse, context = loads.inverse_cross, loads.cross_context
    attend_backward(
        total_of(lengths), WINDOWS_CROSS, loads.cross_queries, loads.mem_keys,
        loads.mem_values, work.probs, inverse, context, lambda rows: nt(branch[rows], weight),
        work.grad_context, work.inner_rows, work.cross_grad, putter(work.key_sum),
        putter(work.value_sum), copies,
    )
    outs.key_low[...] = (work.key_sum[...] + late.mem_key_grad_b[...]).astype(LOW)
    outs.value_low[...] = (work.value_sum[...] + late.mem_value_grad_b[...]).astype(LOW)
    stores.start("key_low", "value_low")
    packs = work.packs
    shipping = Shipping(direct, device, packs, grad_outs, ship_sem)
    weight = matrix(late.weight_query, 0, PER_SIDE)
    grad_second = late.grad_second
    late.unit_one, late.scale_one
    backward_cross_end(
        late, weight, gains, outs.gain_sum, grad_second, work.cross_grad, outs.grad_first,
        outs.self_branch,
    )
    stores.start("grad_first", "self_branch", "gain_sum")
    if direct:
        pack_norms(outs.gain_sum, work.flat, packs, 8, 8)
    put_matrix(
        packs, 0, PER_SIDE,
        tn(late.hidden_one[...], work.cross_grad[...])
        + tn(late.hidden_one_b[...], late.cross_grad_b[...]),
    )
    shipping.send_chip(0)
    put_matrix(packs, 16, PER_SIDE, tn(late.memory[...], outs.key_low[...]))
    shipping.send_chip(1)
    put_matrix(packs, 32, PER_SIDE, tn(late.memory[...], outs.value_low[...]))
    shipping.send_chip(2)
    put_matrix(
        packs, 48, PER_SIDE,
        tn(context[...], branch[...])
        + tn(late.cross_context_b[...], late.cross_branch_b[...]),
    )
    shipping.send_chip(3)
    stores.finish()
    shipping.finish()


class SelfFirst(NamedTuple):
    self_branch: Any = LOW_SQ
    weight_out: Any = MATRIX
    inverse_self: Any = PER_HEAD
    context: Any = LOW_SQ
    keys: Any = LOW_SQ
    values: Any = LOW_SQ
    queries: Any = LOW_SQ


class SelfThen(NamedTuple):
    context_b: Any = LOW_SQ
    self_branch_b: Any = LOW_SQ
    tokens: Any = LOW_SQ
    inputs_b: Any = LOW_SQ
    query_grad_b: Any = LOW_SQ
    key_grad_b: Any = LOW_SQ
    value_grad_b: Any = LOW_SQ


class SelfOuts(NamedTuple):
    query_grad: Any = LOW_SQ
    key_grad: Any = LOW_SQ
    value_grad: Any = LOW_SQ


class SelfWork(NamedTuple):
    probs: Any = PROBS
    grad_context: Any = LOW_SQ
    inner_rows: Any = INNER
    packs: Any = PACKS8
    flat: Any = FLAT


def self_back_kernel(direct, device, lengths, gain_sum, order, also, *refs):
    first_in, probs_in, then_in, targets, grad_outs, first, then, outs, work, sems = split(
        refs, SelfFirst(), 1, SelfThen(), SelfOuts(), 3 if direct else 1, SelfFirst(),
        SelfThen(), SelfOuts(), SelfWork(), 5,
    )
    first_sem, then_sem, probs_sem, out_sem, ship_sem = sems
    stores = Stores(SelfOuts._fields, outs, targets, out_sem)
    loads = Loads(
        SelfFirst._fields, first_in._replace(weight_out=one_matrix(first_in.weight_out, 3)),
        first, first_sem,
    ).start()
    late = Loads(SelfThen._fields, then_in, then, then_sem)
    copies = PairCopies(probs_in[0], work.probs, probs_sem, late)
    branch = loads.self_branch
    weight = matrix(loads.weight_out, 0, PER_SIDE)
    inverse, context = loads.inverse_self, loads.context
    attend_backward(
        total_of(lengths), WINDOWS_SELF, loads.queries, loads.keys, loads.values, work.probs,
        inverse, context, lambda rows: nt(branch[rows], weight), work.grad_context,
        work.inner_rows, outs.query_grad, putter(outs.key_grad), putter(outs.value_grad), copies,
    )
    stores.start(*SelfOuts._fields)
    packs = work.packs
    shipping = Shipping(direct, device, packs, grad_outs, ship_sem)
    if direct:
        pack_norms(gain_sum, work.flat, packs, 0, 8)
    put_matrix(
        packs, 48, PER_SIDE,
        tn(context[...], branch[...]) + tn(late.context_b[...], late.self_branch_b[...]),
    )
    shipping.send_chip(3)
    pairs = (
        (outs.query_grad, late.query_grad_b),
        (outs.key_grad, late.key_grad_b),
        (outs.value_grad, late.value_grad_b),
    )
    for which, (grad, grad_b) in enumerate(pairs):
        put_matrix(
            packs, which * 16, PER_SIDE,
            tn(late.tokens[...], grad[...]) + tn(late.inputs_b[...], grad_b[...]),
        )
        shipping.send_chip(which)
    stores.finish()
    shipping.finish()


class InputGrads(NamedTuple):
    key_low: Any = LOW_SQ
    value_low: Any = LOW_SQ
    wall_cross: Any = ((32 * BLK, BLK), LOW)
    grad_first: Any = F32_SQ
    query_grad: Any = LOW_SQ
    key_grad: Any = LOW_SQ
    value_grad: Any = LOW_SQ
    wall_self: Any = ((48 * BLK, BLK), LOW)


def input_grads_kernel(order, *refs):
    size = len(InputGrads._fields)
    sources, refs = InputGrads(*refs[:size]), refs[size:]
    token_grad, memory_grad = refs[:2]
    targets, sems = refs[2 : 2 + size], refs[2 + size]
    sources = sources._replace(
        wall_cross=sources.wall_cross.at[pl.ds(16 * BLK, 32 * BLK)],
        wall_self=sources.wall_self.at[pl.ds(0, 48 * BLK)],
    )
    loads = Loads(InputGrads._fields, sources, targets, sems).start()
    key_low, value_low, wall = loads.key_low, loads.value_low, loads.wall_cross
    weights = [attn_matrix(wall, which) for which in range(2)]
    for rows in chunks():
        memory_grad[rows] = nt(key_low[rows], weights[0]) + nt(value_low[rows], weights[1])
    grad_first, query_grad, key_grad = loads.grad_first, loads.query_grad, loads.key_grad
    value_grad, wall = loads.value_grad, loads.wall_self
    weights = [attn_matrix(wall, which) for which in range(3)]
    for rows in chunks():
        token_grad[rows] = (
            grad_first[rows]
            + nt(query_grad[rows], weights[0])
            + nt(key_grad[rows], weights[1])
            + nt(value_grad[rows], weights[2])
        )


def shampoo_kernel(grad, weights, graft, left_stat, right_stat, left_root, right_root,
                   new_blocks, new_graft, new_left, new_right):
    for block in range(grad.shape[0]):
        values = grad[block]
        low = values.astype(LOW)
        new_left[block] = STAT_DECAY * left_stat[block] + (1.0 - STAT_DECAY) * nt(low, low)
        new_right[block] = STAT_DECAY * right_stat[block] + (1.0 - STAT_DECAY) * tn(low, low)
        moment = STAT_DECAY * graft[block] + (1.0 - STAT_DECAY) * values * values
        new_graft[block] = moment
        half_way = nn(left_root[block].astype(LOW), low)
        direction = nn(half_way.astype(LOW), right_root[block].astype(LOW))
        adaptive = values / (jnp.sqrt(moment) + GRAFT_EPS)
        ratio = jnp.sqrt(jnp.mean(adaptive * adaptive, keepdims=True)) * lax.rsqrt(
            jnp.mean(direction * direction, keepdims=True) + RATIO_EPS
        )
        new_blocks[block] = weights[block] - BLOCK_RATE * ratio * direction


def shapes_of(*tables):
    return [jax.ShapeDtypeStruct(shape, dtype) for table in tables for shape, dtype in table]


def scratch_of(*tables):
    return [VM(shape, dtype) for table in tables for shape, dtype in table]


def call(kernel, ins, outs, scratch, vmem, busy):
    return pl.pallas_call(
        kernel,
        out_shape=[shape for _, shape in outs],
        in_specs=[pl.BlockSpec(memory_space=space) for space, _ in ins],
        out_specs=[pl.BlockSpec(memory_space=space) for space, _ in outs],
        scratch_shapes=scratch,
        compiler_params=pltpu.CompilerParams(vmem_limit_bytes=vmem),
        cost_estimate=pl.CostEstimate(
            flops=busy * 1_000_000_000 + 1000, bytes_accessed=1000, transcendentals=0
        ),
    )(*[array for _, array in ins])


def inside(space, tables):
    return [(space, shape) for shape in shapes_of(tables)]


class Routes:
    def __init__(self, sides):
        self.sides = sides
        self.places = [
            (z, y, x, core)
            for z in range(sides[0])
            for y in range(sides[1])
            for x in range(sides[2])
            for core in range(2)
        ]

    def index(self, place):
        z, y, x, core = place
        return ((z * self.sides[1] + y) * self.sides[2] + x) * 2 + core

    def move(self, values, step):
        pairs = []
        for place in self.places:
            target = step(*place)
            if target is not None:
                pairs.append((self.index(place), self.index(target)))
        return lax.ppermute(values, AXES, pairs)


def to_core(z, y, x, core):
    return (z, y, x, 1 - core)


def to_x(z, y, x, core):
    return (z, y, 1 - x, core)


def to_y(z, y, x, core):
    return (z, 1 - y, x, core)


def hop_one(z, y, x, core):
    return to_y(z, y, x, core) if core == 0 else to_x(z, y, x, core)


def hop_two(z, y, x, core):
    return to_x(z, y, x, core) if core == 0 else to_y(z, y, x, core)


def ring_z(z, y, x, core):
    return ((z + 1) % 4, y, x, core)


def swap_z(z, y, x, core):
    return (z ^ 1, y, x, core)


def z_onto_high(z, y, x, core):
    return (z + 2, y, x, core) if z < 2 else None


def gather_pieces(routes, packed):
    along = [packed]
    for _ in range(3):
        along.append(routes.move(along[-1], ring_z))
    pieces = []
    for piece in along:
        first = routes.move(piece, hop_one)
        second = routes.move(piece, hop_two)
        third = routes.move(first, hop_two)
        for values in (piece, first, second, third):
            pieces += [values, routes.move(values, to_core)]
    return pieces


PACK = ((PACK_ROWS, BLK), LOW)


def sum_kernel(jobs, term_count, device, *refs):
    terms, out = refs[:term_count], refs[-5]
    parts, sums, sems, out_sems = refs[-4:]
    loads, number = [], 0
    for job in jobs:
        mine = []
        for term, slot, group in job:
            source = terms[term].at[slot, group]
            mine.append(pltpu.make_async_copy(source, parts.at[number], sems.at[number]))
            mine[-1].start()
            number += 1
        loads.append(mine)
    number = 0
    copies = []
    for place, mine in enumerate(loads):
        total = None
        for load in mine:
            load.wait()
            part = parts[number].astype(F32)
            total = part if total is None else total + part
            number += 1
        sums[place] = total.astype(LOW)
        copies.append(
            pltpu.make_async_copy(sums.at[place], out.at[place], out_sems.at[place])
        )
        copies[-1].start()
    for copy in copies:
        copy.wait()


def sum_packs(device, jobs, terms, after=(), busy=3, vmem=PART_VMEM):
    count = sum(len(job) for job in jobs)
    return call(
        functools.partial(sum_kernel, jobs, len(terms)),
        [(pltpu.SMEM, device)] + [(pl.ANY, term) for term in (*terms, *after)],
        [(pl.ANY, jax.ShapeDtypeStruct((len(jobs), PACK_ROWS, BLK), LOW))],
        [VM((count, PACK_ROWS, BLK), LOW), VM((len(jobs), PACK_ROWS, BLK), LOW),
         pltpu.SemaphoreType.DMA((count,)), pltpu.SemaphoreType.DMA((len(jobs),))],
        vmem,
        busy,
    )


def far_sum(routes, device, grads, groups, after=(), vmem=PART_VMEM):
    keep, far_share, near_share = grads
    far_share = routes.move(far_share, to_core)
    near_share = routes.move(near_share, to_core)
    jobs = [
        [(0, 2 + slot, group), (1, slot, group)] for slot in range(2) for group in range(groups)
    ]
    (away,) = sum_packs(device, jobs, [keep, far_share], after, vmem=vmem)
    return away.reshape(2, groups, PACK_ROWS, BLK), [keep, near_share]


def near_job(first, group):
    return [(first, 1, group), (first + 1, 1, group), (first + 2, 1, group)]


def added(*packs):
    total = packs[0].astype(F32)
    for pack in packs[1:]:
        total = total + pack.astype(F32)
    return total


def over_z(routes, away, keep, near_step, far_step):
    total = keep + routes.move(away, near_step).astype(F32)
    return total + routes.move(total.astype(LOW), far_step).astype(F32)


def over_plane(routes, terms, plane):
    def near(z, y, x, core):
        return (z ^ 1, y, x, core) if z % 2 != plane else None

    def far(z, y, x, core):
        return (plane, y, x, core) if z == plane + 2 else None

    away = added(*(term[1, 0] for term in terms)).astype(LOW)
    arrived = routes.move(away, hop_one)
    total = added(*(term[0, 0] for term in terms), arrived)
    return over_z(routes, total.astype(LOW), total, near, far), arrived


def meet(device, *arrived):
    return call(
        lambda *refs: refs[-1].__setitem__(Ellipsis, jnp.zeros((8, BLK), F32)),
        [(pltpu.SMEM, device)] + [(pl.ANY, array) for array in arrived],
        [(VM, jax.ShapeDtypeStruct((8, BLK), F32))],
        [],
        SMALL_VMEM,
        30,
    )


def shards(
    sides,
    tokens,
    memory,
    cotangent,
    lengths,
    blocks,
    norm_params,
    graft_state,
    left_stat,
    right_stat,
    left_root,
    right_root,
    norm_graft,
):
    direct = sides is not None
    blocks_low = blocks.astype(LOW).reshape(-1, BLK)
    norms_low = norm_params.astype(LOW)
    gains_in = []
    if direct:
        routes = Routes(sides)
        norm_rows = jnp.pad(norms_low[None], ((0, 15), (0, BLK - OWN_NORMS)))
        pieces = gather_pieces(routes, jnp.concatenate([blocks_low, norm_rows], axis=0))
    else:
        gains = lax.all_gather(norms_low, AXES, axis=0, tiled=True)
        gains_in = [jnp.pad(gains.astype(F32).reshape(6, D), ((0, 2), (0, 0)))]
        pieces = [lax.all_gather(blocks_low, AXES, axis=0, tiled=True)]

    device = lax.axis_index(AXES).astype(jnp.int32).reshape(1)
    smem, vmem, far = pltpu.SMEM, VM, pl.ANY
    square = jax.ShapeDtypeStruct((TOK_DEV, D), F32)
    square_low = jax.ShapeDtypeStruct((TOK_DEV, D), LOW)
    small = jax.ShapeDtypeStruct((8, D), F32)
    dma = pltpu.SemaphoreType.DMA
    ships = 3 if direct else 1

    def shipped(groups):
        return [(far, shape) for shape in grad_shapes(direct, groups)]

    def far_ins(table, found):
        return [(far, found[name]) for name in table._fields]

    outs = call(
        functools.partial(layers_kernel, direct, len(pieces)),
        [(smem, device), (smem, lengths), (far, tokens), (far, memory), (far, cotangent)]
        + [(vmem, gains) for gains in gains_in]
        + [(far, piece) for piece in pieces],
        [(vmem, square_low), (vmem, small), (vmem, small)] + shipped(2) + inside(far, Saved()),
        scratch_of(Held(), BothApps(), PerApp(), PerApp(), Branches())
        + [dma((2 * len(pieces),)), dma((3,)), dma((len(Saved()),)), dma((16,))],
        MAIN_VMEM,
        50,
    )
    decoded, gains, gain_sum = outs[:3]
    grads_mix = outs[3 : 3 + ships]
    found = dict(zip(Saved._fields, outs[3 + ships :]))
    found.update(memory=memory, tokens=tokens)

    order = [device]
    if direct:
        away, mix = far_sum(routes, device, grads_mix, 2)
        order = [away]
        mix.append(routes.move(away, hop_two))
    found.update(weight_out=found["wall_cross"], weight_query=found["wall_cross"])
    outs = call(
        functools.partial(cross_back_kernel, direct),
        [(smem, device), (smem, lengths), (vmem, gains), (vmem, gain_sum), (far, order[0])]
        + far_ins(CrossFirst, found) + [(far, found["probs_cross"])]
        + far_ins(CrossThen, found),
        inside(far, CrossOuts()) + shipped(1),
        scratch_of(CrossFirst(), CrossThen(), CrossOuts(), CrossWork())
        + [dma((len(CrossFirst()),)), dma((len(CrossThen()),)), dma((PAIRS,)),
           dma((len(CrossOuts()),)), dma((8,))],
        PART_VMEM,
        11,
    )
    found.update(zip(CrossOuts._fields, outs))
    grads_cross = outs[len(CrossOuts()) :]

    order = [device] * 2
    if direct:
        order = [
            sum_packs(device, [near_job(0, group) for group in range(2)], mix, busy=30)[0]
        ]
        away, cross = far_sum(routes, device, grads_cross, 1, order)
        order.append(away)
        mix.append(routes.move(order[0], hop_one)[None])
        cross.append(routes.move(order[1], hop_two))
    found.update(weight_out=found["wall_self"])
    outs = call(
        functools.partial(self_back_kernel, direct),
        [(smem, device), (smem, lengths), (vmem, found["gain_sum"]), (far, order[0]),
         (far, order[1])]
        + far_ins(SelfFirst, found) + [(far, found["probs_self"])]
        + far_ins(SelfThen, found),
        inside(far, SelfOuts()) + shipped(1),
        scratch_of(SelfFirst(), SelfThen(), SelfOuts(), SelfWork())
        + [dma((len(SelfFirst()),)), dma((len(SelfThen()),)), dma((PAIRS,)),
           dma((len(SelfOuts()),)), dma((8,))],
        PART_VMEM,
        10,
    )
    found.update(zip(SelfOuts._fields, outs))
    grads_self = outs[len(SelfOuts()) :]

    order = device
    if direct:
        order, own = far_sum(
            routes, device, grads_self, 1, meet(device, mix[3], cross[2]), SMALL_VMEM
        )
        own.append(routes.move(order, hop_two))
    token_grad, memory_grad = call(
        input_grads_kernel,
        [(far, order)] + far_ins(InputGrads, found),
        [(vmem, square)] * 2,
        scratch_of(InputGrads()) + [dma((len(InputGrads()),))],
        SMALL_VMEM,
        5,
    )

    if direct:
        z = device[0] // (OWNERS // sides[0])
        odd = z % 2 == 1
        own_sum, _ = over_plane(routes, own, 0)
        cross_sum, arrived = over_plane(routes, cross, 1)
        (nothing,) = meet(device, arrived)
        even_sum, odd_sum = [
            added(*(term[0, group] for term in mix)) + nothing[0, 0] for group in range(2)
        ]
        mix_sum = over_z(
            routes, jnp.where(odd, even_sum, odd_sum).astype(LOW),
            jnp.where(odd, odd_sum, even_sum), swap_z, z_onto_high,
        )
        pack = jnp.where(z >= 2, mix_sum, jnp.where(z == 1, cross_sum, own_sum))
        block_grad = pack[:OWN_ROWS].reshape(blocks.shape)
        norm_grad = pack[OWN_ROWS, :OWN_NORMS]
    else:
        terms = jnp.concatenate([grads_self[0], grads_cross[0], grads_mix[0]], axis=0)
        terms = terms.reshape(OWNERS, PACK_ROWS, BLK)[:, :OWN_ROWS].reshape(-1, BLK, BLK)
        block_grad = lax.psum_scatter(
            terms.astype(F32), AXES, scatter_dimension=0, tiled=True
        )
        norm_grad = lax.psum_scatter(
            found["gain_sum"][:6].reshape(-1), AXES, scatter_dimension=0, tiled=True
        )

    updates = (block_grad, blocks, graft_state, left_stat, right_stat, left_root, right_root)
    stack = jax.ShapeDtypeStruct(blocks.shape, F32)
    new_blocks, new_graft, new_left, new_right = call(
        shampoo_kernel, [(vmem, array) for array in updates], [(vmem, stack)] * 4, [],
        14 * 2**20, 5,
    )
    norm_moment = STAT_DECAY * norm_graft + (1.0 - STAT_DECAY) * norm_grad * norm_grad
    new_norms = norm_params - NORM_RATE * norm_grad / (jnp.sqrt(norm_moment) + GRAFT_EPS)
    return (
        decoded,
        token_grad,
        memory_grad,
        block_grad,
        new_blocks,
        new_graft,
        new_left,
        new_right,
        norm_grad,
        new_norms,
        norm_moment,
    )


def solution(mesh):
    rows = P(AXES, None)
    stack = P(AXES, None, None)
    flat = P(AXES)
    sides = GRIDS.get(mesh.shape["dp"]) if mesh.shape["rep"] == 2 else None
    return jax.shard_map(
        functools.partial(shards, sides),
        mesh=mesh,
        in_specs=(rows, rows, rows, rows, stack, flat, stack, stack, stack, stack, stack, flat),
        out_specs=(rows, rows, rows, stack, stack, stack, stack, stack, flat, flat, flat),
        check_vma=False,
    )
```

```python
import functools
from typing import Any, NamedTuple

import jax
import jax.numpy as jnp
from jax import lax
from jax.experimental import pallas as pl
from jax.experimental.pallas import tpu as pltpu
from jax.sharding import PartitionSpec as P

D = 512
HEADS = 8
FF = 2048
BLK = 128
TOK_DEV = 512
PER_SIDE = D // BLK
PANELS = FF // D
PAIRS = HEADS // 2
HALF = 256

STAT_DECAY = 0.5
BLOCK_RATE = 0.05
NORM_RATE = 0.2
NORM_EPS = 1e-05
GRAFT_EPS = 1e-08
RATIO_EPS = 1e-06
MASKED = -1e30
SCALE = (D // HEADS) ** (-0.5)

AXES = ("dp", "rep")
F32 = jnp.float32
LOW = jnp.bfloat16
MAIN_VMEM = 60 * 2**20
PART_VMEM = 63 * 2**20 + 2**19
SMALL_VMEM = 16 * 2**20

GRIDS = {16: (4, 2, 2)}

OWNERS = 32
OWN_BLOCKS = 8
OWN_NORMS = 96
OWN_ROWS = OWN_BLOCKS * BLK
PACK_ROWS = OWN_ROWS + 16

VM = pltpu.VMEM
WINDOWS_SELF = ((0, 256), (128, 384))
WINDOWS_CROSS = ((0, 512), (128, 384))
WINDOWS_ALL = ((0, 512), (0, 512))


def dot(left_mat, right_mat, left_dim, right_dim):
    return lax.dot_general(
        left_mat,
        right_mat,
        (((left_dim,), (right_dim,)), ((), ())),
        preferred_element_type=F32,
    )


def nn(left_mat, right_mat):
    return dot(left_mat, right_mat, 1, 0)


def nt(left_mat, right_mat):
    return dot(left_mat, right_mat, 1, 1)


def tn(left_mat, right_mat):
    return dot(left_mat, right_mat, 0, 0)


def matrix(wall, base, stride):
    def block(number):
        return wall[number * BLK : (number + 1) * BLK]

    rows = [
        jnp.concatenate([block(base + i * stride + j) for j in range(PER_SIDE)], axis=1)
        for i in range(PER_SIDE)
    ]
    return jnp.concatenate(rows, axis=0)


def attn_matrix(wall, which):
    return matrix(wall, which * PER_SIDE * PER_SIDE, PER_SIDE)


def up_panel(wall, panel):
    return matrix(wall, 128 + panel * PER_SIDE, FF // BLK)


def down_panel(wall, panel):
    return matrix(wall, 192 + panel * PER_SIDE * PER_SIDE, PER_SIDE)


def put_matrix(packs, base, stride, values):
    values = values.astype(packs.dtype)
    for i in range(PER_SIDE):
        for j in range(PER_SIDE):
            owner, place = divmod(base + i * stride + j, OWN_BLOCKS)
            first = owner * PACK_ROWS + place * BLK
            packs[first : first + BLK] = values[i * BLK : (i + 1) * BLK, j * BLK : (j + 1) * BLK]


def lanes_below(count, rows=1):
    return lax.broadcasted_iota(jnp.int32, (rows, BLK), 1) < count


def unpack_norms(packed, gains):
    turned = {shift: pltpu.roll(packed, shift, 1) for shift in (32, 64, 96)}
    turned[0] = packed
    for row in range(6 * D // BLK):
        owner, offset = divmod(row * BLK, OWN_NORMS)
        kept = OWN_NORMS - offset
        values = jnp.where(
            lanes_below(kept),
            turned[-offset % BLK][owner : owner + 1],
            turned[kept][owner + 1 : owner + 2],
        )
        gains[row // 4 : row // 4 + 1, (row % 4) * BLK : (row % 4 + 1) * BLK] = values


def pack_norms(gain_sum, flat, packs, first_owner, owners):
    for row in range(6 * D // BLK):
        flat[row : row + 1] = gain_sum[
            row // 4 : row // 4 + 1, (row % 4) * BLK : (row % 4 + 1) * BLK
        ]
    flat[24:32] = jnp.zeros((8, BLK), F32)
    values = flat[...]
    turned = {shift: pltpu.roll(values, shift, 1) for shift in (32, 64, 96)}
    turned[0] = values
    top = lax.broadcasted_iota(jnp.int32, (16, BLK), 0) == 0
    for owner in range(owners):
        row, offset = divmod((first_owner + owner) * OWN_NORMS, BLK)
        source = turned[-offset % BLK]
        mine = jnp.where(
            lanes_below(BLK - offset), source[row : row + 1], source[row + 1 : row + 2]
        )
        last = owner * PACK_ROWS + OWN_ROWS
        packs[last : last + 16] = jnp.where(top, mine, 0.0).astype(packs.dtype)


def norm_forward(values, gain, bias):
    center = values - jnp.mean(values, axis=1, keepdims=True)
    spread = jnp.mean(center * center, axis=1, keepdims=True)
    scale = lax.rsqrt(spread + NORM_EPS)
    unit = center * scale
    return unit * gain + bias, unit, scale


def norm_backward(grad, unit, scale, gain):
    inner = grad * gain
    first = jnp.mean(inner, axis=1, keepdims=True)
    second = jnp.mean(inner * unit, axis=1, keepdims=True)
    grad_in = (inner - first - unit * second) * scale
    grad_gain = jnp.sum(grad * unit, axis=0, keepdims=True)
    grad_bias = jnp.sum(grad, axis=0, keepdims=True)
    return grad_in, grad_gain, grad_bias


def chunks():
    return [pl.ds(start, HALF) for start in range(0, TOK_DEV, HALF)]


def pick_half(values, side):
    lane = lax.broadcasted_iota(jnp.int32, values.shape, 1)
    mine = lane < D // HEADS if side == 0 else lane >= D // HEADS
    return jnp.where(mine, values, jnp.zeros_like(values))


def both_halves(values, axis=0):
    return jnp.concatenate([pick_half(values, 0), pick_half(values, 1)], axis=axis)


def heads_wide(narrow):
    head_of = lax.broadcasted_iota(jnp.int32, (BLK, D), 1) // (D // HEADS)
    chooser = (head_of == lax.broadcasted_iota(jnp.int32, (BLK, D), 0)).astype(F32).astype(LOW)
    high = narrow.astype(LOW)
    rest = (narrow - high.astype(F32)).astype(LOW)
    return nn(
        jnp.concatenate([high, rest], axis=1), jnp.concatenate([chooser, chooser], axis=0)
    )


def for_pairs(total, windows, pair_step, copies=None):
    @pl.when(total >= BLK)
    def _():
        for pair in range(PAIRS):
            if copies is not None:
                copies.wait(pair)
            pair_step(windows, pair, pl.ds(pair * BLK, BLK))

    @pl.when(total < BLK)
    def _():
        if copies is not None:
            for pair in range(PAIRS):
                copies.wait(pair)

        def step(pair, carry):
            pair_step(WINDOWS_ALL, pair, pl.ds(pl.multiple_of(pair * BLK, BLK), BLK))
            return carry

        lax.fori_loop(0, PAIRS, step, 0)


def attend_forward(
    total, windows, queries, key_rows, value_rows, bias, probs, raw, inverse, context
):
    inverse[...] = jnp.zeros_like(inverse)

    def pair_step(spans, pair, lanes):
        for part, (start, size) in enumerate(spans):
            rows = pl.ds(part * HALF, HALF)
            span = pl.ds(start, size)
            query = queries[rows, lanes]
            keys = key_rows[span, lanes]
            values = value_rows[span, lanes]
            lane = lax.broadcasted_iota(jnp.int32, (size, BLK), 1)
            scores = [nt(keys, pick_half(query, side)) for side in range(2)]
            weights, sources = [], []
            for side in range(2):
                masked = scores[side] + bias[span, rows]
                top = jnp.max(masked, axis=0, keepdims=True)
                weight = jnp.exp(masked - top).astype(LOW)
                probs[2 * pair + side, span, rows] = weight
                weights.append(weight)
                ones = (lane == 2 * pair + side).astype(F32).astype(LOW)
                sources.append(jnp.concatenate([pick_half(values, side), ones], axis=1))
            mixed = tn(jnp.concatenate(weights, axis=0), jnp.concatenate(sources, axis=0))
            raw[rows, lanes] = mixed[:, :BLK]
            inverse[rows] += mixed[:, BLK:]

    for_pairs(total, windows, pair_step)
    for rows in chunks():
        sums = inverse[rows]
        narrow = jnp.where(sums > 0.0, 1.0 / sums, 0.0)
        inverse[rows] = narrow
        context[rows] = (raw[rows] * heads_wide(narrow)).astype(LOW)


def attend_backward(
    total, windows, queries, key_rows, value_rows, probs, inverse, context, grad_of,
    grad_context, inner_rows, grad_queries, put_keys, put_values, copies=None,
):
    head_of = lax.broadcasted_iota(jnp.int32, (16, D), 1) // (D // HEADS)
    chooser = (head_of == lax.broadcasted_iota(jnp.int32, (16, D), 0)).astype(F32).astype(LOW)
    for rows in chunks():
        grad = (grad_of(rows) * heads_wide(inverse[rows])).astype(LOW)
        grad_context[rows] = grad
        inner = grad.astype(F32) * context[rows].astype(F32)
        high = inner.astype(LOW)
        rest = (inner - high.astype(F32)).astype(LOW)
        inner_rows[:, rows] = nt(chooser, high) + nt(chooser, rest)

    def pair_step(spans, pair, lanes):
        shares = []
        for part, (start, size) in enumerate(spans):
            rows = pl.ds(part * HALF, HALF)
            span = pl.ds(start, size)
            keys = key_rows[span, lanes]
            values = value_rows[span, lanes]
            grad = grad_context[rows, lanes]
            weights = [probs[2 * pair + side, span, rows] for side in range(2)]
            grad_probs = [nt(values, pick_half(grad, side)) for side in range(2)]
            slopes = []
            for side in range(2):
                base = inner_rows[pl.ds(2 * pair + side, 1), rows]
                slopes.append((weights[side].astype(F32) * (grad_probs[side] - base)).astype(LOW))
            grad_queries[rows, lanes] = (
                tn(jnp.concatenate(slopes, axis=0), both_halves(keys)) * SCALE
            ).astype(LOW)
            shares.append(
                (
                    nn(jnp.concatenate(slopes, axis=1), both_halves(queries[rows, lanes])),
                    nn(jnp.concatenate(weights, axis=1), both_halves(grad)),
                )
            )
        for first in range(0, TOK_DEV, BLK):
            rows = pl.ds(first, BLK)
            for which, put in enumerate((put_keys, put_values)):
                parts = [
                    share[which][first - start : first - start + BLK]
                    for share, (start, size) in zip(shares, spans)
                    if start <= first < start + size
                ]
                put(rows, lanes, sum(parts[1:], parts[0]))

    for_pairs(total, windows, pair_step, copies)


def putter(target):
    def put(rows, lanes, values):
        target[rows, lanes] = values.astype(target.dtype)

    return put


def total_of(lengths):
    total = lengths[0, 0]
    for number in range(1, lengths.shape[1]):
        total = total + lengths[0, number]
    return total


def place_of(device):
    number = device[0]
    return number >> 3, (number >> 2) & 1, (number >> 1) & 1, number & 1


def make_biases(lengths, bias_self, bias_cross):
    count = lengths.shape[1]
    row = lax.broadcasted_iota(jnp.int32, (32, 1), 0)
    low = jnp.zeros((32, 1), jnp.int32)
    high = jnp.zeros((32, 1), jnp.int32)
    bound = jnp.int32(0)
    for number in range(count):
        low = jnp.where(row == number, bound, low)
        bound = bound + lengths[0, number]
        high = jnp.where(row == number, bound, high)
    low = jnp.where(row == count, bound, low)
    high = jnp.where(row == count, TOK_DEV, high)
    slot = lax.broadcasted_iota(jnp.int32, (32, TOK_DEV), 1)
    member = ((slot >= low) & (slot < high)).astype(F32).astype(LOW)
    for rows in chunks():
        apart = (tn(member, member[:, rows.start : rows.start + HALF]) - 1.0) * -MASKED
        key = lax.broadcasted_iota(jnp.int32, apart.shape, 0)
        query = lax.broadcasted_iota(jnp.int32, apart.shape, 1) + rows.start
        bias_cross[:, rows] = apart
        bias_self[:, rows] = jnp.where(key <= query, apart, MASKED)


class Shipping:
    def __init__(self, direct, device, packs, outs, sems):
        self.direct, self.packs, self.outs, self.sems = direct, packs, outs, sems
        _, self.y, self.x, self.core = place_of(device)
        self.waits = []

    def send(self, group, chip, core):
        number = (group * 4 + chip) * 2 + core
        source = self.packs.at[pl.ds(number * PACK_ROWS, PACK_ROWS)]
        sem = self.sems.at[number]
        if not self.direct:
            target = self.outs[0].at[pl.ds(number * PACK_ROWS, PACK_ROWS)]
            self.waits.append(pltpu.make_async_copy(source, target, sem))
            self.waits[-1].start()
            return
        move_y, move_x = self.y ^ (chip >> 1), self.x ^ (chip & 1)
        slot = move_x * 2 + move_y if core == 0 else move_y * 2 + move_x
        keep = pltpu.make_async_copy(source, self.outs[0].at[slot, group], sem)
        side = slot & 1

        @pl.when(self.core == core)
        def _():
            keep.start()

        @pl.when((self.core != core) & (slot >= 2))
        def _():
            pltpu.make_async_copy(source, self.outs[1].at[side, group], sem).start()

        @pl.when((self.core != core) & (slot < 2))
        def _():
            pltpu.make_async_copy(source, self.outs[2].at[side, group], sem).start()

        self.waits.append(keep)

    def send_chip(self, chip):
        for core in range(2):
            self.send(0, chip, core)

    def finish(self):
        for copy in self.waits:
            copy.wait()


def grad_shapes(direct, groups):
    if direct:
        return [
            jax.ShapeDtypeStruct((slots, groups, PACK_ROWS, BLK), LOW) for slots in (4, 2, 2)
        ]
    return [jax.ShapeDtypeStruct((groups * 8 * PACK_ROWS, BLK), LOW)]


LOW_SQ = ((TOK_DEV, D), LOW)
F32_SQ = ((TOK_DEV, D), F32)
COLUMN = ((TOK_DEV, 1), F32)
PER_HEAD = ((TOK_DEV, BLK), F32)
PROBS = ((HEADS, TOK_DEV, TOK_DEV), LOW)
WALL64 = ((64 * BLK, BLK), LOW)
PACKS8 = ((8 * PACK_ROWS, BLK), LOW)
WIDE = ((TOK_DEV, FF), LOW)
GAINS = ((8, D), F32)
INNER = ((16, TOK_DEV), F32)
FLAT = ((32, BLK), F32)


class Saved(NamedTuple):
    wall_self: Any = WALL64
    wall_cross: Any = WALL64
    probs_self: Any = PROBS
    probs_cross: Any = PROBS
    inverse_self: Any = PER_HEAD
    inverse_cross: Any = PER_HEAD
    queries: Any = LOW_SQ
    keys: Any = LOW_SQ
    values: Any = LOW_SQ
    context: Any = LOW_SQ
    hidden_one: Any = LOW_SQ
    cross_queries: Any = LOW_SQ
    cross_context: Any = LOW_SQ
    unit_one: Any = F32_SQ
    scale_one: Any = COLUMN
    mem_keys: Any = LOW_SQ
    mem_values: Any = LOW_SQ
    grad_second: Any = F32_SQ
    cross_branch: Any = LOW_SQ
    inputs_b: Any = LOW_SQ
    context_b: Any = LOW_SQ
    hidden_one_b: Any = LOW_SQ
    cross_context_b: Any = LOW_SQ
    cross_branch_b: Any = LOW_SQ
    cross_grad_b: Any = LOW_SQ
    self_branch_b: Any = LOW_SQ
    query_grad_b: Any = LOW_SQ
    key_grad_b: Any = LOW_SQ
    value_grad_b: Any = LOW_SQ
    mem_key_grad_b: Any = F32_SQ
    mem_value_grad_b: Any = F32_SQ


class Held(NamedTuple):
    tokens: Any = LOW_SQ
    memory: Any = LOW_SQ
    cotangent: Any = LOW_SQ
    bias_self: Any = F32_SQ
    bias_cross: Any = F32_SQ
    wall: Any = ((256 * BLK, BLK), LOW)
    norms: Any = ((OWNERS, 16, BLK), LOW)
    flat: Any = FLAT
    probs_self: Any = PROBS
    probs_cross: Any = PROBS
    inverse_self: Any = PER_HEAD
    inverse_cross: Any = PER_HEAD
    mem_keys: Any = LOW_SQ
    mem_values: Any = LOW_SQ
    state: Any = F32_SQ
    hidden: Any = F32_SQ
    grad_context: Any = LOW_SQ
    inner_rows: Any = INNER
    key_sum: Any = F32_SQ
    value_sum: Any = F32_SQ
    grad_second: Any = F32_SQ


class BothApps(NamedTuple):
    inputs: Any = LOW_SQ
    queries: Any = LOW_SQ
    keys: Any = LOW_SQ
    values: Any = LOW_SQ
    context: Any = LOW_SQ
    unit_one: Any = F32_SQ
    scale_one: Any = COLUMN
    hidden_one: Any = LOW_SQ
    cross_queries: Any = LOW_SQ
    cross_context: Any = LOW_SQ


class PerApp(NamedTuple):
    unit_two: Any = F32_SQ
    scale_two: Any = COLUMN
    hidden_two: Any = LOW_SQ
    gelu_slope: Any = WIDE
    activated: Any = WIDE
    unit_three: Any = F32_SQ
    scale_three: Any = COLUMN
    down_branch: Any = LOW_SQ


class Branches(NamedTuple):
    cross_branch: Any = LOW_SQ
    cross_grad: Any = LOW_SQ
    self_branch: Any = LOW_SQ
    query_grad: Any = LOW_SQ
    key_grad: Any = LOW_SQ
    value_grad: Any = LOW_SQ


def gelu_parts(values):
    first = 0.7978845608028654
    cubic = 0.044715 * first
    square = values * values
    bend = jnp.tanh(values * (first + cubic * square))
    half = 0.5 + 0.5 * bend
    slope = half + (0.5 * values) * (1.0 - bend * bend) * (first + (3.0 * cubic) * square)
    return values * half, slope


def attend_self(app, held, bias, total):
    weights = [attn_matrix(held.wall, which) for which in range(3)]
    for rows in chunks():
        inputs = held.state[rows].astype(LOW)
        app.inputs[rows] = inputs
        app.queries[rows] = (nn(inputs, weights[0]) * SCALE).astype(LOW)
        app.keys[rows] = nn(inputs, weights[1]).astype(LOW)
        app.values[rows] = nn(inputs, weights[2]).astype(LOW)
    attend_forward(
        total, WINDOWS_SELF, app.queries, app.keys, app.values, bias, held.probs_self,
        held.hidden, held.inverse_self, app.context,
    )


def finish_self(app, held, gains):
    weight = attn_matrix(held.wall, 3)
    for rows in chunks():
        total_rows = held.state[rows] + nn(app.context[rows], weight)
        out, unit, scale = norm_forward(total_rows, gains[0:1], gains[1:2])
        app.unit_one[rows] = unit
        app.scale_one[rows] = scale
        app.hidden_one[rows] = out.astype(LOW)
        held.hidden[rows] = out


def forward_cross(app, held, gains, bias, total):
    weight = attn_matrix(held.wall, 4)
    for rows in chunks():
        app.cross_queries[rows] = (nn(app.hidden_one[rows], weight) * SCALE).astype(LOW)
    attend_forward(
        total, WINDOWS_CROSS, app.cross_queries, held.mem_keys, held.mem_values, bias,
        held.probs_cross, held.state, held.inverse_cross, app.cross_context,
    )
    weight = attn_matrix(held.wall, 7)
    for rows in chunks():
        total_rows = held.hidden[rows] + nn(app.cross_context[rows], weight)
        out, unit, scale = norm_forward(total_rows, gains[2:3], gains[3:4])
        app.unit_two[rows] = unit
        app.scale_two[rows] = scale
        app.hidden_two[rows] = out.astype(LOW)
        held.hidden[rows] = out


def forward_mix(app, held, gains, finish):
    for rows in chunks():
        mixed = app.hidden_two[rows]
        total_rows = held.hidden[rows]
        for panel in range(PANELS):
            lanes = pl.ds(panel * D, D)
            active, slope = gelu_parts(nn(mixed, up_panel(held.wall, panel)))
            active = active.astype(LOW)
            app.activated[rows, lanes] = active
            app.gelu_slope[rows, lanes] = slope.astype(LOW)
            total_rows = total_rows + nn(active, down_panel(held.wall, panel))
        out, unit, scale = norm_forward(total_rows, gains[4:5], gains[5:6])
        app.unit_three[rows] = unit
        app.scale_three[rows] = scale
        finish(rows, out)


def backward_mix(app, held, gains, gain_sum, grad_of, branch):
    for rows in chunks():
        grad_third, gain3, bias3 = norm_backward(
            grad_of(rows), app.unit_three[rows], app.scale_three[rows], gains[4:5]
        )
        gain_sum[4:5] += gain3
        gain_sum[5:6] += bias3
        grad_low = grad_third.astype(LOW)
        app.down_branch[rows] = grad_low
        for panel in range(PANELS):
            lanes = pl.ds(panel * D, D)
            grad_active = nt(grad_low, down_panel(held.wall, panel))
            grad_pre = (grad_active * app.gelu_slope[rows, lanes].astype(F32)).astype(LOW)
            app.gelu_slope[rows, lanes] = grad_pre
            grad_third = grad_third + nt(grad_pre, up_panel(held.wall, panel))
        grad_in, gain2, bias2 = norm_backward(
            grad_third, app.unit_two[rows], app.scale_two[rows], gains[2:3]
        )
        gain_sum[2:3] += gain2
        gain_sum[3:4] += bias2
        held.grad_second[rows] = grad_in
        branch[rows] = grad_in.astype(LOW)


def backward_cross_end(app, weight, gains, gain_sum, grad_second, cross_grad, grad_first,
                       self_branch):
    for rows in chunks():
        grad = grad_second[rows] + nt(cross_grad[rows], weight)
        grad_in, gain1, bias1 = norm_backward(
            grad, app.unit_one[rows], app.scale_one[rows], gains[0:1]
        )
        gain_sum[0:1] += gain1
        gain_sum[1:2] += bias1
        grad_first[rows] = grad_in
        self_branch[rows] = grad_in.astype(LOW)


def layers_kernel(direct, piece_count, *refs):
    refs = list(refs)

    def take(table):
        count = table if isinstance(table, int) else len(table)
        taken, refs[:count] = refs[:count], []
        return taken if isinstance(table, int) else type(table)(*taken)

    device, lengths, tokens, memory, cotangent = take(5)
    gains_in = [] if direct else take(1)
    pieces = take(piece_count)
    decoded, gains, gain_sum = take(3)
    grad_outs = take(3 if direct else 1)
    saved = take(Saved())
    held = take(Held())
    both = take(BothApps())
    app_a, app_b, branches = take(PerApp()), take(PerApp()), take(Branches())
    piece_sem, input_sem, save_sem, ship_sem = take(4)

    class App(NamedTuple):
        inputs: Any
        queries: Any
        keys: Any
        values: Any
        context: Any
        unit_one: Any
        scale_one: Any
        hidden_one: Any
        cross_queries: Any
        cross_context: Any
        unit_two: Any
        scale_two: Any
        hidden_two: Any
        gelu_slope: Any
        activated: Any
        unit_three: Any
        scale_three: Any
        down_branch: Any

    app_a, app_b = App(*both, *app_a), App(*both, *app_b)
    wall = held.wall
    total = total_of(lengths)
    inputs = [
        pltpu.make_async_copy(source, target, input_sem.at[number])
        for number, (source, target) in enumerate(
            ((tokens, held.tokens), (memory, held.memory), (cotangent, held.cotangent))
        )
    ]
    inputs[0].start()
    if direct:
        arrive = fetch_pieces(device, pieces, wall, held.norms, piece_sem)
    else:
        whole = pltpu.make_async_copy(pieces[0], wall, piece_sem.at[0])
        whole.start()

        def arrive(group):
            if group == 0:
                whole.wait()

    for load in inputs[1:]:
        load.start()
    bias_self, bias_cross = held.bias_self, held.bias_cross
    make_biases(lengths, bias_self, bias_cross)
    gain_sum[...] = jnp.zeros_like(gain_sum)
    inputs[0].wait()
    memory, cotangent = held.memory, held.cotangent
    for rows in chunks():
        held.state[rows] = held.tokens[rows].astype(F32)
    arrive(0)

    stores = {}

    def save(target, source):
        number = len(stores)
        stores[number] = pltpu.make_async_copy(source, target, save_sem.at[number])
        stores[number].start()
        return number

    def settle(numbers):
        for number in numbers:
            stores[number].wait()

    walls = [save(saved.wall_self, wall.at[pl.ds(0, 64 * BLK)])]
    later = []
    gains[6:8] = jnp.zeros((2, D), F32)

    real = {
        start: lax.broadcasted_iota(jnp.int32, (HALF, 1), 0) + start < total
        for start in range(0, TOK_DEV, HALF)
    }

    def keep_state(rows, out):
        held.state[rows] = out

    def keep_decoded(rows, out):
        decoded[rows] = jnp.where(real[rows.start], out, 0.0).astype(LOW)

    attend_self(app_a, held, bias_self, total)
    arrive(1)
    arrive(2)
    arrive(3)
    if direct:
        for owner in range(OWNERS):
            held.flat[owner : owner + 1] = held.norms[owner].astype(F32)[0:1]
        unpack_norms(held.flat[...], gains)
    else:
        gains[...] = gains_in[0][...]
    walls.append(save(saved.wall_cross, wall.at[pl.ds(64 * BLK, 64 * BLK)]))
    for load in inputs[1:]:
        load.wait()
    weights = [attn_matrix(wall, which) for which in (5, 6)]
    for rows in chunks():
        held.mem_keys[rows] = nn(memory[rows], weights[0]).astype(LOW)
        held.mem_values[rows] = nn(memory[rows], weights[1]).astype(LOW)
    later += [save(saved.mem_keys, held.mem_keys), save(saved.mem_values, held.mem_values)]
    finish_self(app_a, held, gains)
    first_saves = [
        save(saved.probs_self, held.probs_self),
        save(saved.inverse_self, held.inverse_self),
        save(saved.queries, app_a.queries),
        save(saved.keys, app_a.keys),
        save(saved.values, app_a.values),
        save(saved.context, app_a.context),
        save(saved.hidden_one, app_a.hidden_one),
        save(saved.unit_one, app_a.unit_one),
        save(saved.scale_one, app_a.scale_one),
    ]
    forward_cross(app_a, held, gains, bias_cross, total)
    second_saves = [
        save(saved.probs_cross, held.probs_cross),
        save(saved.inverse_cross, held.inverse_cross),
        save(saved.cross_queries, app_a.cross_queries),
        save(saved.cross_context, app_a.cross_context),
    ]
    forward_mix(app_a, held, gains, keep_state)
    settle(first_saves)
    attend_self(app_b, held, bias_self, total)
    finish_self(app_b, held, gains)
    settle(second_saves)
    forward_cross(app_b, held, gains, bias_cross, total)
    forward_mix(app_b, held, gains, keep_decoded)
    later += [
        save(saved.inputs_b, app_b.inputs),
        save(saved.context_b, app_b.context),
        save(saved.hidden_one_b, app_b.hidden_one),
        save(saved.cross_context_b, app_b.cross_context),
    ]

    def last_grad(rows):
        return jnp.where(real[rows.start], cotangent[rows].astype(F32), 0.0)

    backward_mix(app_b, held, gains, gain_sum, last_grad, branches.cross_branch)
    later.append(save(saved.cross_branch_b, branches.cross_branch))
    weight = attn_matrix(wall, 7)
    attend_backward(
        total, WINDOWS_CROSS, app_b.cross_queries, held.mem_keys, held.mem_values,
        held.probs_cross, held.inverse_cross, app_b.cross_context,
        lambda rows: nt(branches.cross_branch[rows], weight), held.grad_context,
        held.inner_rows, branches.cross_grad, putter(held.key_sum), putter(held.value_sum),
    )
    later += [
        save(saved.mem_key_grad_b, held.key_sum),
        save(saved.mem_value_grad_b, held.value_sum),
        save(saved.cross_grad_b, branches.cross_grad),
    ]
    backward_cross_end(
        app_b, attn_matrix(wall, 4), gains, gain_sum, held.grad_second, branches.cross_grad,
        held.hidden, branches.self_branch,
    )
    later.append(save(saved.self_branch_b, branches.self_branch))
    weight_out = attn_matrix(wall, 3)
    attend_backward(
        total, WINDOWS_SELF, app_b.queries, app_b.keys, app_b.values, held.probs_self,
        held.inverse_self, app_b.context,
        lambda rows: nt(branches.self_branch[rows], weight_out), held.grad_context,
        held.inner_rows, branches.query_grad, putter(branches.key_grad),
        putter(branches.value_grad),
    )
    later += [
        save(saved.query_grad_b, branches.query_grad),
        save(saved.key_grad_b, branches.key_grad),
        save(saved.value_grad_b, branches.value_grad),
    ]
    weights = [attn_matrix(wall, which) for which in range(3)]
    for rows in chunks():
        held.state[rows] = (
            held.hidden[rows]
            + nt(branches.query_grad[rows], weights[0])
            + nt(branches.key_grad[rows], weights[1])
            + nt(branches.value_grad[rows], weights[2])
        )
    backward_mix(
        app_a, held, gains, gain_sum, lambda rows: held.state[rows], held.grad_context
    )
    later += [
        save(saved.grad_second, held.grad_second),
        save(saved.cross_branch, held.grad_context),
    ]

    settle(walls)
    packs = wall
    if direct:
        pack_norms(gain_sum, held.flat, packs, 16, 16)
    shipping = Shipping(direct, device, packs, grad_outs, ship_sem)
    for panel in range(PANELS):
        lanes = pl.ds(panel * D, D)
        put_matrix(
            packs, panel * PER_SIDE, FF // BLK,
            tn(app_a.hidden_two[...], app_a.gelu_slope[:, lanes])
            + tn(app_b.hidden_two[...], app_b.gelu_slope[:, lanes]),
        )
        if panel % 2 == 1:
            for chip in range(4):
                shipping.send(0, chip, panel // 2)
    for panel in range(PANELS):
        lanes = pl.ds(panel * D, D)
        put_matrix(
            packs, 64 + panel * PER_SIDE * PER_SIDE, PER_SIDE,
            tn(app_a.activated[:, lanes], app_a.down_branch[...])
            + tn(app_b.activated[:, lanes], app_b.down_branch[...]),
        )
        for core in range(2):
            shipping.send(1, panel, core)
    settle(later)
    shipping.finish()


def fetch_pieces(device, pieces, wall, norms, sems):
    z, y, x, core = place_of(device)
    copies = []
    for number, piece in enumerate(pieces):
        back, spot, other = number >> 3, (number >> 1) & 3, number & 1
        one, two = spot & 1, spot >> 1
        lane = core ^ other
        at_y = y ^ jnp.where(lane == 0, one, two)
        at_x = x ^ jnp.where(lane == 0, two, one)
        owner = ((((z - back) & 3) * 2 + at_y) * 2 + at_x) * 2 + lane
        copies.append(
            (
                pltpu.make_async_copy(
                    piece.at[pl.ds(0, OWN_ROWS)],
                    wall.at[pl.ds(pl.multiple_of(owner * OWN_ROWS, OWN_ROWS), OWN_ROWS)],
                    sems.at[2 * number],
                ),
                pltpu.make_async_copy(
                    piece.at[pl.ds(OWN_ROWS, 16)], norms.at[owner], sems.at[2 * number + 1]
                ),
            )
        )
    def for_plane(plane, act):
        for back in range(4):

            @pl.when(((z - plane) & 3) == back)
            def _(back=back):
                for pair in copies[back * 8 : back * 8 + 8]:
                    for copy in pair:
                        act(copy)

    def arrive(plane):
        for_plane(plane, lambda copy: copy.wait())
        if plane == 0:
            for other in range(1, 4):
                for_plane(other, lambda copy: copy.start())

    for_plane(0, lambda copy: copy.start())
    return arrive


class Loads:
    def __init__(self, names, sources, targets, sems):
        self.targets = dict(zip(names, targets))
        self.copies = {
            name: pltpu.make_async_copy(source, target, sems.at[number])
            for number, (name, source, target) in enumerate(zip(names, sources, targets))
        }

    def start(self):
        for copy in self.copies.values():
            copy.start()
        return self

    def __getattr__(self, name):
        if name in self.copies:
            self.copies.pop(name).wait()
        return self.targets[name]


class Stores:
    def __init__(self, names, sources, targets, sems):
        self.copies = {
            name: pltpu.make_async_copy(source, target, sems.at[number])
            for number, (name, source, target) in enumerate(zip(names, sources, targets))
        }

    def start(self, *names):
        for name in names:
            self.copies[name].start()

    def finish(self):
        for copy in self.copies.values():
            copy.wait()


def one_matrix(wall, which):
    return wall.at[pl.ds(which * 16 * BLK, 16 * BLK)]


class PairCopies:
    def __init__(self, source, target, sems, then):
        self.copies = [
            pltpu.make_async_copy(
                source.at[pl.ds(2 * pair, 2)], target.at[pl.ds(2 * pair, 2)], sems.at[pair]
            )
            for pair in range(PAIRS)
        ]
        self.copies[0].start()
        self.then = then

    def wait(self, pair):
        if pair == 0:
            for copy in self.copies[1:]:
                copy.start()
        self.copies[pair].wait()
        if pair == 1:
            self.then.start()


MATRIX = ((16 * BLK, BLK), LOW)


class CrossFirst(NamedTuple):
    cross_branch: Any = LOW_SQ
    weight_out: Any = MATRIX
    inverse_cross: Any = PER_HEAD
    cross_context: Any = LOW_SQ
    mem_keys: Any = LOW_SQ
    mem_values: Any = LOW_SQ
    cross_queries: Any = LOW_SQ


class CrossThen(NamedTuple):
    mem_key_grad_b: Any = F32_SQ
    mem_value_grad_b: Any = F32_SQ
    weight_query: Any = MATRIX
    grad_second: Any = F32_SQ
    unit_one: Any = F32_SQ
    scale_one: Any = COLUMN
    hidden_one: Any = LOW_SQ
    hidden_one_b: Any = LOW_SQ
    cross_grad_b: Any = LOW_SQ
    memory: Any = LOW_SQ
    cross_context_b: Any = LOW_SQ
    cross_branch_b: Any = LOW_SQ


class CrossOuts(NamedTuple):
    grad_first: Any = F32_SQ
    self_branch: Any = LOW_SQ
    gain_sum: Any = GAINS
    key_low: Any = LOW_SQ
    value_low: Any = LOW_SQ


class CrossWork(NamedTuple):
    probs: Any = PROBS
    key_sum: Any = F32_SQ
    value_sum: Any = F32_SQ
    grad_context: Any = LOW_SQ
    inner_rows: Any = INNER
    cross_grad: Any = LOW_SQ
    packs: Any = PACKS8
    flat: Any = FLAT


def split(refs, *parts):
    found, first = [], 0
    for part in parts:
        count = part if isinstance(part, int) else len(part)
        taken = refs[first : first + count]
        found.append(taken if isinstance(part, int) else type(part)(*taken))
        first += count
    return found


def cross_back_kernel(direct, device, lengths, gains, gain_before, order, *refs):
    first_in, probs_in, then_in, targets, grad_outs, first, then, outs, work, sems = split(
        refs, CrossFirst(), 1, CrossThen(), CrossOuts(), 3 if direct else 1, CrossFirst(),
        CrossThen(), CrossOuts(), CrossWork(), 5,
    )
    first_sem, then_sem, probs_sem, out_sem, ship_sem = sems
    stores = Stores(CrossOuts._fields, outs, targets, out_sem)
    loads = Loads(
        CrossFirst._fields, first_in._replace(weight_out=one_matrix(first_in.weight_out, 3)),
        first, first_sem,
    ).start()
    late = Loads(
        CrossThen._fields, then_in._replace(weight_query=one_matrix(then_in.weight_query, 0)),
        then, then_sem,
    )
    copies = PairCopies(probs_in[0], work.probs, probs_sem, late)
    outs.gain_sum[...] = gain_before[...]
    branch = loads.cross_branch
    weight = matrix(loads.weight_out, 0, PER_SIDE)
    inverse, context = loads.inverse_cross, loads.cross_context
    attend_backward(
        total_of(lengths), WINDOWS_CROSS, loads.cross_queries, loads.mem_keys,
        loads.mem_values, work.probs, inverse, context, lambda rows: nt(branch[rows], weight),
        work.grad_context, work.inner_rows, work.cross_grad, putter(work.key_sum),
        putter(work.value_sum), copies,
    )
    outs.key_low[...] = (work.key_sum[...] + late.mem_key_grad_b[...]).astype(LOW)
    outs.value_low[...] = (work.value_sum[...] + late.mem_value_grad_b[...]).astype(LOW)
    stores.start("key_low", "value_low")
    packs = work.packs
    shipping = Shipping(direct, device, packs, grad_outs, ship_sem)
    weight = matrix(late.weight_query, 0, PER_SIDE)
    grad_second = late.grad_second
    late.unit_one, late.scale_one
    backward_cross_end(
        late, weight, gains, outs.gain_sum, grad_second, work.cross_grad, outs.grad_first,
        outs.self_branch,
    )
    stores.start("grad_first", "self_branch", "gain_sum")
    if direct:
        pack_norms(outs.gain_sum, work.flat, packs, 8, 8)
    put_matrix(
        packs, 0, PER_SIDE,
        tn(late.hidden_one[...], work.cross_grad[...])
        + tn(late.hidden_one_b[...], late.cross_grad_b[...]),
    )
    shipping.send_chip(0)
    put_matrix(packs, 16, PER_SIDE, tn(late.memory[...], outs.key_low[...]))
    shipping.send_chip(1)
    put_matrix(packs, 32, PER_SIDE, tn(late.memory[...], outs.value_low[...]))
    shipping.send_chip(2)
    put_matrix(
        packs, 48, PER_SIDE,
        tn(context[...], branch[...])
        + tn(late.cross_context_b[...], late.cross_branch_b[...]),
    )
    shipping.send_chip(3)
    stores.finish()
    shipping.finish()


class SelfFirst(NamedTuple):
    self_branch: Any = LOW_SQ
    weight_out: Any = MATRIX
    inverse_self: Any = PER_HEAD
    context: Any = LOW_SQ
    keys: Any = LOW_SQ
    values: Any = LOW_SQ
    queries: Any = LOW_SQ


class SelfThen(NamedTuple):
    context_b: Any = LOW_SQ
    self_branch_b: Any = LOW_SQ
    tokens: Any = LOW_SQ
    inputs_b: Any = LOW_SQ
    query_grad_b: Any = LOW_SQ
    key_grad_b: Any = LOW_SQ
    value_grad_b: Any = LOW_SQ


class SelfOuts(NamedTuple):
    query_grad: Any = LOW_SQ
    key_grad: Any = LOW_SQ
    value_grad: Any = LOW_SQ


class SelfWork(NamedTuple):
    probs: Any = PROBS
    grad_context: Any = LOW_SQ
    inner_rows: Any = INNER
    packs: Any = PACKS8
    flat: Any = FLAT


def self_back_kernel(direct, device, lengths, gain_sum, order, also, *refs):
    first_in, probs_in, then_in, targets, grad_outs, first, then, outs, work, sems = split(
        refs, SelfFirst(), 1, SelfThen(), SelfOuts(), 3 if direct else 1, SelfFirst(),
        SelfThen(), SelfOuts(), SelfWork(), 5,
    )
    first_sem, then_sem, probs_sem, out_sem, ship_sem = sems
    stores = Stores(SelfOuts._fields, outs, targets, out_sem)
    loads = Loads(
        SelfFirst._fields, first_in._replace(weight_out=one_matrix(first_in.weight_out, 3)),
        first, first_sem,
    ).start()
    late = Loads(SelfThen._fields, then_in, then, then_sem)
    copies = PairCopies(probs_in[0], work.probs, probs_sem, late)
    branch = loads.self_branch
    weight = matrix(loads.weight_out, 0, PER_SIDE)
    inverse, context = loads.inverse_self, loads.context
    attend_backward(
        total_of(lengths), WINDOWS_SELF, loads.queries, loads.keys, loads.values, work.probs,
        inverse, context, lambda rows: nt(branch[rows], weight), work.grad_context,
        work.inner_rows, outs.query_grad, putter(outs.key_grad), putter(outs.value_grad), copies,
    )
    stores.start(*SelfOuts._fields)
    packs = work.packs
    shipping = Shipping(direct, device, packs, grad_outs, ship_sem)
    if direct:
        pack_norms(gain_sum, work.flat, packs, 0, 8)
    put_matrix(
        packs, 48, PER_SIDE,
        tn(context[...], branch[...]) + tn(late.context_b[...], late.self_branch_b[...]),
    )
    shipping.send_chip(3)
    pairs = (
        (outs.query_grad, late.query_grad_b),
        (outs.key_grad, late.key_grad_b),
        (outs.value_grad, late.value_grad_b),
    )
    for which, (grad, grad_b) in enumerate(pairs):
        put_matrix(
            packs, which * 16, PER_SIDE,
            tn(late.tokens[...], grad[...]) + tn(late.inputs_b[...], grad_b[...]),
        )
        shipping.send_chip(which)
    stores.finish()
    shipping.finish()


class InputGrads(NamedTuple):
    key_low: Any = LOW_SQ
    value_low: Any = LOW_SQ
    wall_cross: Any = ((32 * BLK, BLK), LOW)
    grad_first: Any = F32_SQ
    query_grad: Any = LOW_SQ
    key_grad: Any = LOW_SQ
    value_grad: Any = LOW_SQ
    wall_self: Any = ((48 * BLK, BLK), LOW)


def input_grads_kernel(order, *refs):
    size = len(InputGrads._fields)
    sources, refs = InputGrads(*refs[:size]), refs[size:]
    token_grad, memory_grad = refs[:2]
    targets, sems = refs[2 : 2 + size], refs[2 + size]
    sources = sources._replace(
        wall_cross=sources.wall_cross.at[pl.ds(16 * BLK, 32 * BLK)],
        wall_self=sources.wall_self.at[pl.ds(0, 48 * BLK)],
    )
    loads = Loads(InputGrads._fields, sources, targets, sems).start()
    key_low, value_low, wall = loads.key_low, loads.value_low, loads.wall_cross
    weights = [attn_matrix(wall, which) for which in range(2)]
    for rows in chunks():
        memory_grad[rows] = nt(key_low[rows], weights[0]) + nt(value_low[rows], weights[1])
    grad_first, query_grad, key_grad = loads.grad_first, loads.query_grad, loads.key_grad
    value_grad, wall = loads.value_grad, loads.wall_self
    weights = [attn_matrix(wall, which) for which in range(3)]
    for rows in chunks():
        token_grad[rows] = (
            grad_first[rows]
            + nt(query_grad[rows], weights[0])
            + nt(key_grad[rows], weights[1])
            + nt(value_grad[rows], weights[2])
        )


def shampoo_kernel(grad, weights, graft, left_stat, right_stat, left_root, right_root,
                   new_blocks, new_graft, new_left, new_right):
    for block in range(grad.shape[0]):
        values = grad[block]
        low = values.astype(LOW)
        new_left[block] = STAT_DECAY * left_stat[block] + (1.0 - STAT_DECAY) * nt(low, low)
        new_right[block] = STAT_DECAY * right_stat[block] + (1.0 - STAT_DECAY) * tn(low, low)
        moment = STAT_DECAY * graft[block] + (1.0 - STAT_DECAY) * values * values
        new_graft[block] = moment
        half_way = nn(left_root[block].astype(LOW), low)
        direction = nn(half_way.astype(LOW), right_root[block].astype(LOW))
        adaptive = values / (jnp.sqrt(moment) + GRAFT_EPS)
        ratio = jnp.sqrt(jnp.mean(adaptive * adaptive, keepdims=True)) * lax.rsqrt(
            jnp.mean(direction * direction, keepdims=True) + RATIO_EPS
        )
        new_blocks[block] = weights[block] - BLOCK_RATE * ratio * direction


def shapes_of(*tables):
    return [jax.ShapeDtypeStruct(shape, dtype) for table in tables for shape, dtype in table]


def scratch_of(*tables):
    return [VM(shape, dtype) for table in tables for shape, dtype in table]


def call(kernel, ins, outs, scratch, vmem, busy):
    return pl.pallas_call(
        kernel,
        out_shape=[shape for _, shape in outs],
        in_specs=[pl.BlockSpec(memory_space=space) for space, _ in ins],
        out_specs=[pl.BlockSpec(memory_space=space) for space, _ in outs],
        scratch_shapes=scratch,
        compiler_params=pltpu.CompilerParams(vmem_limit_bytes=vmem),
        cost_estimate=pl.CostEstimate(
            flops=busy * 1_000_000_000 + 1000, bytes_accessed=1000, transcendentals=0
        ),
    )(*[array for _, array in ins])


def inside(space, tables):
    return [(space, shape) for shape in shapes_of(tables)]


class Routes:
    def __init__(self, sides):
        self.sides = sides
        self.places = [
            (z, y, x, core)
            for z in range(sides[0])
            for y in range(sides[1])
            for x in range(sides[2])
            for core in range(2)
        ]

    def index(self, place):
        z, y, x, core = place
        return ((z * self.sides[1] + y) * self.sides[2] + x) * 2 + core

    def move(self, values, step):
        pairs = []
        for place in self.places:
            target = step(*place)
            if target is not None:
                pairs.append((self.index(place), self.index(target)))
        return lax.ppermute(values, AXES, pairs)


def to_core(z, y, x, core):
    return (z, y, x, 1 - core)


def to_x(z, y, x, core):
    return (z, y, 1 - x, core)


def to_y(z, y, x, core):
    return (z, 1 - y, x, core)


def hop_one(z, y, x, core):
    return to_y(z, y, x, core) if core == 0 else to_x(z, y, x, core)


def hop_two(z, y, x, core):
    return to_x(z, y, x, core) if core == 0 else to_y(z, y, x, core)


def ring_z(z, y, x, core):
    return ((z + 1) % 4, y, x, core)


def swap_z(z, y, x, core):
    return (z ^ 1, y, x, core)


def z_onto_high(z, y, x, core):
    return (z + 2, y, x, core) if z < 2 else None


def gather_pieces(routes, packed):
    along = [packed]
    for _ in range(3):
        along.append(routes.move(along[-1], ring_z))
    pieces = []
    for piece in along:
        first = routes.move(piece, hop_one)
        second = routes.move(piece, hop_two)
        third = routes.move(first, hop_two)
        for values in (piece, first, second, third):
            pieces += [values, routes.move(values, to_core)]
    return pieces


PACK = ((PACK_ROWS, BLK), LOW)


def sum_kernel(jobs, term_count, device, *refs):
    terms, out = refs[:term_count], refs[-5]
    parts, sums, sems, out_sems = refs[-4:]
    loads, number = [], 0
    for job in jobs:
        mine = []
        for term, slot, group in job:
            source = terms[term].at[slot, group]
            mine.append(pltpu.make_async_copy(source, parts.at[number], sems.at[number]))
            mine[-1].start()
            number += 1
        loads.append(mine)
    number = 0
    copies = []
    for place, mine in enumerate(loads):
        total = None
        for load in mine:
            load.wait()
            part = parts[number].astype(F32)
            total = part if total is None else total + part
            number += 1
        sums[place] = total.astype(LOW)
        copies.append(
            pltpu.make_async_copy(sums.at[place], out.at[place], out_sems.at[place])
        )
        copies[-1].start()
    for copy in copies:
        copy.wait()


def sum_packs(device, jobs, terms, after=(), busy=3, vmem=PART_VMEM):
    count = sum(len(job) for job in jobs)
    return call(
        functools.partial(sum_kernel, jobs, len(terms)),
        [(pltpu.SMEM, device)] + [(pl.ANY, term) for term in (*terms, *after)],
        [(pl.ANY, jax.ShapeDtypeStruct((len(jobs), PACK_ROWS, BLK), LOW))],
        [VM((count, PACK_ROWS, BLK), LOW), VM((len(jobs), PACK_ROWS, BLK), LOW),
         pltpu.SemaphoreType.DMA((count,)), pltpu.SemaphoreType.DMA((len(jobs),))],
        vmem,
        busy,
    )


def far_sum(routes, device, grads, groups, after=(), vmem=PART_VMEM):
    keep, far_share, near_share = grads
    far_share = routes.move(far_share, to_core)
    near_share = routes.move(near_share, to_core)
    jobs = [
        [(0, 2 + slot, group), (1, slot, group)] for slot in range(2) for group in range(groups)
    ]
    (away,) = sum_packs(device, jobs, [keep, far_share], after, vmem=vmem)
    return away.reshape(2, groups, PACK_ROWS, BLK), [keep, near_share]


def near_job(first, group):
    return [(first, 1, group), (first + 1, 1, group), (first + 2, 1, group)]


def added(*packs):
    total = packs[0].astype(F32)
    for pack in packs[1:]:
        total = total + pack.astype(F32)
    return total


def over_z(routes, away, keep, near_step, far_step):
    total = keep + routes.move(away, near_step).astype(F32)
    return total + routes.move(total.astype(LOW), far_step).astype(F32)


def over_plane(routes, terms, plane):
    def near(z, y, x, core):
        return (z ^ 1, y, x, core) if z % 2 != plane else None

    def far(z, y, x, core):
        return (plane, y, x, core) if z == plane + 2 else None

    away = added(*(term[1, 0] for term in terms)).astype(LOW)
    arrived = routes.move(away, hop_one)
    total = added(*(term[0, 0] for term in terms), arrived)
    return over_z(routes, total.astype(LOW), total, near, far), arrived


def meet(device, *arrived):
    return call(
        lambda *refs: refs[-1].__setitem__(Ellipsis, jnp.zeros((8, BLK), F32)),
        [(pltpu.SMEM, device)] + [(pl.ANY, array) for array in arrived],
        [(VM, jax.ShapeDtypeStruct((8, BLK), F32))],
        [],
        SMALL_VMEM,
        30,
    )


def shards(
    sides,
    tokens,
    memory,
    cotangent,
    lengths,
    blocks,
    norm_params,
    graft_state,
    left_stat,
    right_stat,
    left_root,
    right_root,
    norm_graft,
):
    direct = sides is not None
    blocks_low = blocks.astype(LOW).reshape(-1, BLK)
    norms_low = norm_params.astype(LOW)
    gains_in = []
    if direct:
        routes = Routes(sides)
        norm_rows = jnp.pad(
            norm_params[None], ((OWN_ROWS, 15), (0, BLK - OWN_NORMS))
        )
        packed = (jnp.pad(blocks.reshape(-1, BLK), ((0, 16), (0, 0))) + norm_rows).astype(LOW)
        pieces = gather_pieces(routes, packed)
    else:
        gains = lax.all_gather(norms_low, AXES, axis=0, tiled=True)
        gains_in = [jnp.pad(gains.astype(F32).reshape(6, D), ((0, 2), (0, 0)))]
        pieces = [lax.all_gather(blocks_low, AXES, axis=0, tiled=True)]

    device = lax.axis_index(AXES).astype(jnp.int32).reshape(1)
    smem, vmem, far = pltpu.SMEM, VM, pl.ANY
    square = jax.ShapeDtypeStruct((TOK_DEV, D), F32)
    square_low = jax.ShapeDtypeStruct((TOK_DEV, D), LOW)
    small = jax.ShapeDtypeStruct((8, D), F32)
    dma = pltpu.SemaphoreType.DMA
    ships = 3 if direct else 1

    def shipped(groups):
        return [(far, shape) for shape in grad_shapes(direct, groups)]

    def far_ins(table, found):
        return [(far, found[name]) for name in table._fields]

    outs = call(
        functools.partial(layers_kernel, direct, len(pieces)),
        [(smem, device), (smem, lengths), (far, tokens), (far, memory), (far, cotangent)]
        + [(vmem, gains) for gains in gains_in]
        + [(far, piece) for piece in pieces],
        [(vmem, square_low), (vmem, small), (vmem, small)] + shipped(2) + inside(far, Saved()),
        scratch_of(Held(), BothApps(), PerApp(), PerApp(), Branches())
        + [dma((2 * len(pieces),)), dma((3,)), dma((len(Saved()),)), dma((16,))],
        MAIN_VMEM,
        50,
    )
    decoded, gains, gain_sum = outs[:3]
    grads_mix = outs[3 : 3 + ships]
    found = dict(zip(Saved._fields, outs[3 + ships :]))
    found.update(memory=memory, tokens=tokens)

    order = [device]
    if direct:
        away, mix = far_sum(routes, device, grads_mix, 2)
        order = [away]
        mix.append(routes.move(away, hop_two))
    found.update(weight_out=found["wall_cross"], weight_query=found["wall_cross"])
    outs = call(
        functools.partial(cross_back_kernel, direct),
        [(smem, device), (smem, lengths), (vmem, gains), (vmem, gain_sum), (far, order[0])]
        + far_ins(CrossFirst, found) + [(far, found["probs_cross"])]
        + far_ins(CrossThen, found),
        inside(far, CrossOuts()) + shipped(1),
        scratch_of(CrossFirst(), CrossThen(), CrossOuts(), CrossWork())
        + [dma((len(CrossFirst()),)), dma((len(CrossThen()),)), dma((PAIRS,)),
           dma((len(CrossOuts()),)), dma((8,))],
        PART_VMEM,
        11,
    )
    found.update(zip(CrossOuts._fields, outs))
    grads_cross = outs[len(CrossOuts()) :]

    order = [device] * 2
    if direct:
        order = [
            sum_packs(device, [near_job(0, group) for group in range(2)], mix, busy=30)[0]
        ]
        away, cross = far_sum(routes, device, grads_cross, 1, order)
        order.append(away)
        mix.append(routes.move(order[0], hop_one)[None])
        cross.append(routes.move(order[1], hop_two))
    found.update(weight_out=found["wall_self"])
    outs = call(
        functools.partial(self_back_kernel, direct),
        [(smem, device), (smem, lengths), (vmem, found["gain_sum"]), (far, order[0]),
         (far, order[1])]
        + far_ins(SelfFirst, found) + [(far, found["probs_self"])]
        + far_ins(SelfThen, found),
        inside(far, SelfOuts()) + shipped(1),
        scratch_of(SelfFirst(), SelfThen(), SelfOuts(), SelfWork())
        + [dma((len(SelfFirst()),)), dma((len(SelfThen()),)), dma((PAIRS,)),
           dma((len(SelfOuts()),)), dma((8,))],
        PART_VMEM,
        10,
    )
    found.update(zip(SelfOuts._fields, outs))
    grads_self = outs[len(SelfOuts()) :]

    order = device
    if direct:
        order, own = far_sum(
            routes, device, grads_self, 1, meet(device, mix[3], cross[2]), SMALL_VMEM
        )
        own.append(routes.move(order, hop_two))
    token_grad, memory_grad = call(
        input_grads_kernel,
        [(far, order)] + far_ins(InputGrads, found),
        [(vmem, square)] * 2,
        scratch_of(InputGrads()) + [dma((len(InputGrads()),))],
        SMALL_VMEM,
        5,
    )

    if direct:
        z = device[0] // (OWNERS // sides[0])
        odd = z % 2 == 1
        own_sum, _ = over_plane(routes, own, 0)
        cross_sum, arrived = over_plane(routes, cross, 1)
        (nothing,) = meet(device, arrived)
        even_sum, odd_sum = [
            added(*(term[0, group] for term in mix)) + nothing[0, 0] for group in range(2)
        ]
        mix_sum = over_z(
            routes, jnp.where(odd, even_sum, odd_sum).astype(LOW),
            jnp.where(odd, odd_sum, even_sum), swap_z, z_onto_high,
        )
        pack = jnp.where(z >= 2, mix_sum, jnp.where(z == 1, cross_sum, own_sum))
        block_grad = pack[:OWN_ROWS].reshape(blocks.shape)
        norm_grad = pack[OWN_ROWS, :OWN_NORMS]
    else:
        terms = jnp.concatenate([grads_self[0], grads_cross[0], grads_mix[0]], axis=0)
        terms = terms.reshape(OWNERS, PACK_ROWS, BLK)[:, :OWN_ROWS].reshape(-1, BLK, BLK)
        block_grad = lax.psum_scatter(
            terms.astype(F32), AXES, scatter_dimension=0, tiled=True
        )
        norm_grad = lax.psum_scatter(
            found["gain_sum"][:6].reshape(-1), AXES, scatter_dimension=0, tiled=True
        )

    updates = (block_grad, blocks, graft_state, left_stat, right_stat, left_root, right_root)
    stack = jax.ShapeDtypeStruct(blocks.shape, F32)
    new_blocks, new_graft, new_left, new_right = call(
        shampoo_kernel, [(vmem, array) for array in updates], [(vmem, stack)] * 4, [],
        14 * 2**20, 5,
    )
    norm_moment = STAT_DECAY * norm_graft + (1.0 - STAT_DECAY) * norm_grad * norm_grad
    new_norms = norm_params - NORM_RATE * norm_grad / (jnp.sqrt(norm_moment) + GRAFT_EPS)
    return (
        decoded,
        token_grad,
        memory_grad,
        block_grad,
        new_blocks,
        new_graft,
        new_left,
        new_right,
        norm_grad,
        new_norms,
        norm_moment,
    )


def solution(mesh):
    rows = P(AXES, None)
    stack = P(AXES, None, None)
    flat = P(AXES)
    sides = GRIDS.get(mesh.shape["dp"]) if mesh.shape["rep"] == 2 else None
    return jax.shard_map(
        functools.partial(shards, sides),
        mesh=mesh,
        in_specs=(rows, rows, rows, rows, stack, flat, stack, stack, stack, stack, stack, flat),
        out_specs=(rows, rows, rows, stack, stack, stack, stack, stack, flat, flat, flat),
        check_vma=False,
    )
```
